512 devices in a mesh: seq: 64 (over y_lo, z, x), tp: 8 (over y_hi, core).
Axes of the slice: x: 4, y: 8 (y_hi: 4, y_lo: 2; y = y_hi * 2 + y_lo), z: 8, core: 2. Of those that a mesh axis runs over, the one named last changes fastest.
Arguments:
- query_act: bfloat16 [16384, 3072], P('seq', 'tp'), may hold values from -1200 to 1200
- key_act: bfloat16 [16384, 3072], P('seq', 'tp'), may hold values from -1200 to 1200
- value_act: bfloat16 [16384, 3072], P('seq', 'tp'), may hold values from -26 to 26
- hidden_act: bfloat16 [16384, 10240], P('seq', 'tp'), may hold values from -19 to 19
- conv_weight: float32 [27, 10240], P(None, 'tp'), may hold values from -1.25 to 1.25
- attention_grad: bfloat16 [16384, 3072], P('seq', 'tp'), may hold values from -26 to 26
- feedforward_grad: bfloat16 [16384, 10240], P('seq', 'tp'), may hold values from -6 to 6
Outputs:
- attention_out: bfloat16 [16384, 3072], P('seq', 'tp')
- feedforward_out: bfloat16 [16384, 10240], P('seq', 'tp')
- grad_query: bfloat16 [16384, 3072], P('seq', 'tp')
- grad_key: bfloat16 [16384, 3072], P('seq', 'tp')
- grad_value: bfloat16 [16384, 3072], P('seq', 'tp')
- grad_hidden: bfloat16 [16384, 10240], P('seq', 'tp')
The draws below stay inside these ranges and needn't reach their ends.
All inputs are finite; a program needn't handle non-finite values.
Results may differ from the reference program's by a relative error of at most 0.0049.
Values may be sent and summed in bfloat16 or wider, within the bound.
A program may use at most 64 MiB of HBM per device.

```python
import jax
import jax.numpy as jnp
from jax import lax

HEADS = 24
HD = 128
FFC = 10240
HGT = 8
WID = 16
TOK_DEV = 256
TOKENS = 16384


def column_profile(key, count):
    spread = jax.random.uniform(key, (count,), jnp.float32)
    trend = jnp.sqrt(1.0 + 2.0 * jnp.arange(count, dtype=jnp.float32) / (count - 1))
    return 10.0 ** spread * trend


def row_trend(count):
    return 1.0 + 2.0 * jnp.arange(count, dtype=jnp.float32) / (count - 1)


def shared_normal(key, salt, count):
    return jax.random.truncated_normal(jax.random.fold_in(key, salt), -6.0, 6.0, (TOKENS, count), jnp.float32)


def block_offsets(key, count):
    block_count = TOKENS // TOK_DEV
    key_phase, key_jitter = jax.random.split(key)
    phase = jax.random.uniform(key_phase, (1, count), jnp.float32, 0.0, 2.0 * jnp.pi)
    place = (jnp.arange(block_count, dtype=jnp.float32) + 0.5) / block_count
    wave = 1.2 * jnp.cos(2.0 * jnp.pi * place[:, None] + phase)
    jitter = jax.random.uniform(key_jitter, (block_count, count), jnp.float32, -0.6, 0.6)
    return jnp.repeat(wave + jitter, TOK_DEV, axis=0)


def block_factors(key):
    block_count = TOKENS // TOK_DEV
    key_sign, key_mag = jax.random.split(key)
    flipped = jax.random.bernoulli(key_sign, 0.5, (block_count,))
    level = jax.random.uniform(key_mag, (block_count,), jnp.float32)
    factor = jnp.where(flipped, -(0.2 + 0.25 * level), 0.7 + 0.3 * level)
    return jnp.repeat(factor, TOK_DEV)


def draw_query_act(key, part):
    shared = shared_normal(key, 101, HEADS * HD)
    key = jax.random.fold_in(key, 1)
    key_rows, key_cols = jax.random.split(key)
    row_scales = 10.0 ** jax.random.uniform(key_rows, (TOKENS, 1), jnp.float32)
    profile = column_profile(key_cols, HEADS * HD)
    result = shared * profile[None, :] * row_scales
    return result.astype(jnp.bfloat16)


def draw_key_act(key, part):
    shared = shared_normal(key, 102, HEADS * HD)
    key = jax.random.fold_in(key, 2)
    key_rows, key_cols, key_blocks = jax.random.split(key, 3)
    row_scales = 10.0 ** jax.random.uniform(key_rows, (TOKENS, 1), jnp.float32)
    profile = column_profile(key_cols, HEADS * HD)
    offsets = block_offsets(key_blocks, HEADS * HD)
    result = (shared + offsets) * profile[None, :] * row_scales
    result = jnp.clip(result, -1200.0, 1200.0)
    return result.astype(jnp.bfloat16)


def draw_value_act(key, part):
    shared = shared_normal(key, 102, HEADS * HD)
    key = jax.random.fold_in(key, 3)
    key_noise = jax.random.fold_in(key, 0)
    noise = jax.random.truncated_normal(key_noise, -6.0, 6.0, (TOKENS, HEADS * HD), jnp.float32)
    result = (0.6 * jnp.roll(shared, 37, axis=1) + 0.8 * noise) * row_trend(TOKENS)[:, None]
    return result.astype(jnp.bfloat16)


def draw_attention_grad(key, part):
    shared = shared_normal(key, 101, HEADS * HD)
    key = jax.random.fold_in(key, 4)
    key_noise = jax.random.fold_in(key, 0)
    key_blocks = jax.random.fold_in(key, 2)
    factors = block_factors(key_blocks)
    noise = jax.random.truncated_normal(key_noise, -6.0, 6.0, (TOKENS, HEADS * HD), jnp.float32)
    result = (0.6 * jnp.roll(shared, 37, axis=1) + 0.8 * noise) * (row_trend(TOKENS) * factors)[:, None]
    return result.astype(jnp.bfloat16)


def draw_hidden_act(key, part):
    key = jax.random.fold_in(key, 5)
    key_noise = jax.random.fold_in(key, 0)
    noise = jax.random.truncated_normal(key_noise, -6.0, 6.0, (TOKENS, FFC), jnp.float32)
    result = noise * row_trend(TOKENS)[:, None]
    return result.astype(jnp.bfloat16)


def level_of(stream_key, extent, pieces, low, largest):
    level, own = 1.0, jax.random.fold_in(stream_key, 6)
    for axis_at, blocks in pieces:
        steps = jnp.exp(jax.random.uniform(jax.random.fold_in(own, axis_at), (blocks,), jnp.float32, low / len(pieces), largest / len(pieces)))
        level = level * jnp.repeat(steps, extent[axis_at] // blocks).reshape([-1 if axis == axis_at else 1 for axis in range(len(extent))])
    return level


def normal_values(stream_key, shape, width, most, cuts=(), kind=jnp.bfloat16):
    drawn = jax.random.normal(stream_key, shape, jnp.float32) * width
    if len(cuts) > 0:
        drawn = level_of(stream_key, shape, cuts, -0.22, 0.18) * drawn
    return jnp.clip(drawn, min=-most, max=most).astype(kind)


def setup_inputs(seed: int = 0) -> dict:
    streams_of = jax.random.split(jax.random.key(seed), 8)
    return {
        "query_act": draw_query_act(jax.random.fold_in(streams_of[7], 71), 0),
        "key_act": draw_key_act(jax.random.fold_in(streams_of[7], 71), 0),
        "value_act": draw_value_act(jax.random.fold_in(streams_of[7], 71), 0),
        "hidden_act": draw_hidden_act(jax.random.fold_in(streams_of[7], 71), 0),
        "conv_weight": normal_values(streams_of[4], (27, FFC), 27 ** -0.5, 1.25, ((1, 8),), jnp.float32),
        "attention_grad": draw_attention_grad(jax.random.fold_in(streams_of[7], 71), 0),
        "feedforward_grad": normal_values(streams_of[6], (TOKENS, FFC), 1.0, 6.0, ((0, 64), (1, 8))),
    }


EPS = 1e-06
PRECISE = lax.Precision.HIGHEST

def unit_features(raw_values):
    row_scale = jnp.sqrt(lax.optimization_barrier(jnp.mean(raw_values * raw_values, axis=1)) + EPS)
    return (jnp.maximum(raw_values, 0.0) / row_scale[:, None], row_scale)

def norm_backward(raw_values, features, row_scale, grad_feat, feature_count):
    inner_sum = lax.optimization_barrier(jnp.sum(features * grad_feat, axis=1))
    direct = jnp.where(raw_values > 0, grad_feat, 0.0) / row_scale[:, None]
    result = direct - (inner_sum / (feature_count * row_scale * row_scale))[:, None] * raw_values
    return result.astype(jnp.bfloat16)

def tap_sum(padded, weight, mirror):
    frames = padded.shape[0] - 2
    height = padded.shape[1] - 2
    breadth = padded.shape[2] - 2
    running = jnp.zeros((frames, height, breadth, padded.shape[3]), jnp.float32)
    for frame_off in range(3):
        for row_off in range(3):
            for col_off in range(3):
                tap_index = frame_off * 9 + row_off * 3 + col_off
                if mirror:
                    first_f, first_r, first_c = (2 - frame_off, 2 - row_off, 2 - col_off)
                else:
                    first_f, first_r, first_c = (frame_off, row_off, col_off)
                window = padded[first_f:first_f + frames, first_r:first_r + height, first_c:first_c + breadth]
                running = running + weight[tap_index] * window.astype(jnp.float32)
    return running

def conv_block(operands):
    hidden_block, grad_block, weight_block = operands
    widths = ((1, 1), (1, 1), (1, 1), (0, 0))
    pre_act = tap_sum(jnp.pad(hidden_block, widths), weight_block, False)
    sigmoid_pre = jax.nn.sigmoid(pre_act)
    activated = (pre_act * sigmoid_pre).astype(jnp.bfloat16)
    grad_pre = (grad_block.astype(jnp.float32) * sigmoid_pre * (1.0 + pre_act * (1.0 - sigmoid_pre))).astype(jnp.bfloat16)
    grad_in = tap_sum(jnp.pad(grad_pre, widths), weight_block, True).astype(jnp.bfloat16)
    return (activated, grad_in)

def reference(query_act, key_act, value_act, hidden_act, conv_weight, attention_grad, feedforward_grad):
    feature_count = HEADS * HD
    query_vals = query_act.astype(jnp.float32)
    key_vals = key_act.astype(jnp.float32)
    feat_query, scale_query = unit_features(query_vals)
    feat_key, scale_key = unit_features(key_vals)
    query3 = feat_query.reshape(TOKENS, HEADS, HD)
    keys3 = feat_key.reshape(TOKENS, HEADS, HD)
    value3 = value_act.astype(jnp.float32).reshape(TOKENS, HEADS, HD)
    kv_total = jnp.einsum('thi,thj->hij', keys3, value3, precision=PRECISE) / TOKENS
    norm_total = lax.optimization_barrier(jnp.sum(keys3, axis=0)) / TOKENS
    numerator = jnp.einsum('thi,hij->thj', query3, kv_total, precision=PRECISE)
    denominator = 1.0 + jnp.einsum('thi,hi->th', query3, norm_total, precision=PRECISE) / HD
    attention = numerator / denominator[:, :, None]
    attention_out = attention.reshape(TOKENS, feature_count).astype(jnp.bfloat16)
    grad3 = attention_grad.astype(jnp.float32).reshape(TOKENS, HEADS, HD)
    grad_numer = grad3 / denominator[:, :, None]
    grad_denom = -lax.optimization_barrier(jnp.sum(grad3 * attention, axis=2)) / denominator / HD
    grad_fq = jnp.einsum('thj,hij->thi', grad_numer, kv_total, precision=PRECISE) + grad_denom[:, :, None] * norm_total[None]
    kv_grad = jnp.einsum('thi,thj->hij', query3, grad_numer, precision=PRECISE) / TOKENS
    norm_grad = jnp.einsum('th,thi->hi', grad_denom, query3, precision=PRECISE) / TOKENS
    grad_fk = jnp.einsum('thj,hij->thi', value3, kv_grad, precision=PRECISE) + norm_grad[None]
    grad_value = jnp.einsum('thi,hij->thj', keys3, kv_grad, precision=PRECISE)
    grad_value = grad_value.reshape(TOKENS, feature_count).astype(jnp.bfloat16)
    grad_query = norm_backward(query_vals, feat_query, scale_query, grad_fq.reshape(TOKENS, feature_count), feature_count)
    grad_key = norm_backward(key_vals, feat_key, scale_key, grad_fk.reshape(TOKENS, feature_count), feature_count)
    block_cols = 128 if FFC % 128 == 0 else FFC
    blocks = FFC // block_cols
    frames_all = TOKENS // (HGT * WID)
    hidden5 = hidden_act.reshape(frames_all, HGT, WID, blocks, block_cols).transpose(3, 0, 1, 2, 4)
    grad5 = feedforward_grad.reshape(frames_all, HGT, WID, blocks, block_cols).transpose(3, 0, 1, 2, 4)
    weight3 = conv_weight.reshape(27, blocks, block_cols).transpose(1, 0, 2)
    activated, grad_in = lax.map(conv_block, (hidden5, grad5, weight3))
    feedforward_out = activated.transpose(1, 2, 3, 0, 4).reshape(TOKENS, FFC)
    grad_hidden = grad_in.transpose(1, 2, 3, 0, 4).reshape(TOKENS, FFC)
    return (attention_out, feedforward_out, grad_query, grad_key, grad_value, grad_hidden)
```

```python
import functools

import jax
import jax.numpy as jnp
from jax import lax
from jax.experimental import pallas as pl
from jax.experimental.pallas import tpu as pltpu
from jax.sharding import PartitionSpec as P

HEADS = 24
HD = 128
HGT = 8
WID = 16
EPS = 1e-06

F32 = jnp.float32
BF16 = jnp.bfloat16

TOK = 256
FRAME = HGT * WID
HEADS_DEV = 3
COLS = HEADS_DEV * HD
CHAN = 1280
PAD_ROWS = FRAME + 2 * WID
FEATURES = HEADS * HD
TOKENS = 16384

NX, NZ, NYL = 4, 8, 2
NYH, NCORE = 4, 2
PLANE = NX * NYL
CHUNK = COLS // PLANE
HALO_COLS = 256
HALO_PARTS = CHAN // HALO_COLS
SEQ = NX * NZ * NYL
VMEM_LIMIT = 58 * 1024 * 1024


def nn(a, b):
    return lax.dot_general(a, b, (((1,), (0,)), ((), ())), preferred_element_type=F32)


def nt(a, b):
    return lax.dot_general(a, b, (((1,), (1,)), ((), ())), preferred_element_type=F32)


def tn(a, b):
    return lax.dot_general(a, b, (((0,), (0,)), ((), ())), preferred_element_type=F32)


def row_sums(x):
    ones = jnp.ones((8, x.shape[1]), BF16)
    high, low = split(x)
    return nt(ones, high) + nt(ones, low)


def as_columns(rows, first, count):
    lane = lax.broadcasted_iota(jnp.int32, (8, count * HD), 1) // HD
    row = lax.broadcasted_iota(jnp.int32, (8, count * HD), 0)
    pick = jnp.where(row == lane + first, 1.0, 0.0).astype(F32)
    return lax.dot_general(
        rows, pick, (((0,), (0,)), ((), ())), preferred_element_type=F32, precision=lax.Precision.HIGHEST
    )


def split(x):
    high = x.astype(BF16)
    return high, (x - high.astype(F32)).astype(BF16)


def head(i):
    return pl.ds(i * HD, HD)


def kernel(
    q_in, k_in, v_in, g_in, h_in, fg_in, w_in,
    att_out, ff_out, gq_out, gk_out, gv_out, gh_out,
    q, k, v, g, fg, w, hp, gp,
    att_o, ff_o, gq_o, gk_o, gv_o, gh_o,
    fq, fql, fk, gn, gnl, rinv, dinv, gden, gfk,
    tp1, tp2, tp3,
    kvp, kvs, kv1, kvc, kv2, kvb,
    gkp, gks, gk1, gkc, gk2, gkb,
    z1, z2, zt, gz1, gz2, gzt,
    in_sem, out_sem,
    tp_send, tp_recv, plane_send, plane_recv, ring_send, ring_recv,
    halo_send, halo_recv,
):
    s = lax.axis_index("seq")
    t = lax.axis_index("tp")
    yl, z, x = s // (NZ * NX), (s // NX) % NZ, s % NX
    yh, core = t // NCORE, t % NCORE

    def seq_at(yl_, z_, x_):
        return (yl_ * NZ + z_) * NX + x_

    def plane_at(j):
        return (yl + j // NX) % NYL, (x + j % NX) % NX

    def plane_dev(j):
        yl_, x_ = plane_at(j)
        return {"seq": seq_at(yl_, z, x_), "tp": t}

    def ring_dev(j):
        return {"seq": seq_at(yl, (z + j) % NZ, x), "tp": t}

    def tp_dev(j):
        return {"seq": s, "tp": ((yh + j // NCORE) % NYH) * NCORE + (core + j % NCORE) % NCORE}

    def remote(src, dst, send, recv, device):
        return pltpu.make_async_remote_copy(
            src_ref=src, dst_ref=dst, send_sem=send, recv_sem=recv,
            device_id=device, device_id_type=pl.DeviceIdType.MESH,
        )

    me = yl * NX + x
    mine = pl.ds(pl.multiple_of(me * CHUNK, 16), CHUNK)

    def plane_rows(j):
        yl_, x_ = plane_at(j)
        return pl.ds(pl.multiple_of((yl_ * NX + x_) * CHUNK, 16), CHUNK)

    def tp_round(i, buf):
        return [remote(buf.at[0], buf.at[j], tp_send.at[i, j], tp_recv.at[i, j], tp_dev(j)) for j in range(1, 8)]

    def ring_round(i, src, dst):
        return [remote(src, dst.at[j], ring_send.at[i, j], ring_recv.at[i, j], ring_dev(j)) for j in range(1, NZ)]

    def plane_round(i, src, dst):
        return [remote(src, dst.at[j], plane_send.at[i, j], plane_recv.at[i, j], plane_dev(j)) for j in range(1, PLANE)]

    def plane_scatter(i, src, dst):
        return [
            remote(src.at[plane_rows(j)], dst.at[j], plane_send.at[i, j], plane_recv.at[i, j], plane_dev(j))
            for j in range(1, PLANE)
        ]

    def plane_gather(i, buf):
        return [
            remote(buf.at[mine], buf.at[mine], plane_send.at[i, j], plane_recv.at[i, j], plane_dev(j))
            for j in range(1, PLANE)
        ]

    sent = []

    def start(copies):
        for copy in copies:
            copy.start()
        sent.extend(copies)

    def arrived(copies):
        for copy in copies:
            copy.wait_recv()

    def total(own, buf, count):
        for j in range(1, count):
            own = own + buf[j].astype(F32)
        return own

    up = {"seq": (s + 1) % SEQ, "tp": t}
    down = {"seq": (s + SEQ - 1) % SEQ, "tp": t}
    body_rows = pl.ds(WID, FRAME)

    def halo_copies(i, part, buf, src_up, src_down):
        cols = pl.ds(part * HALO_COLS, HALO_COLS)
        to_next = remote(
            src_up(cols), buf.at[0, body_rows, cols], halo_send.at[i, 0, part], halo_recv.at[i, 0, part], up
        )
        to_prev = remote(
            src_down(cols), buf.at[3, body_rows, cols], halo_send.at[i, 1, part], halo_recv.at[i, 1, part], down
        )
        return to_next, to_prev

    def hidden_halo(part):
        return halo_copies(
            0, part, hp, lambda c: h_in.at[pl.ds(FRAME, FRAME), c], lambda c: h_in.at[pl.ds(0, FRAME), c]
        )

    def grad_halo(part):
        return halo_copies(1, part, gp, lambda c: gp.at[2, body_rows, c], lambda c: gp.at[1, body_rows, c])

    def halo_start(copies):
        @pl.when(s < SEQ - 1)
        def _():
            copies[0].start()

        @pl.when(s > 0)
        def _():
            copies[1].start()

    def halo_arrived(copies):
        @pl.when(s > 0)
        def _():
            copies[0].wait_recv()

        @pl.when(s < SEQ - 1)
        def _():
            copies[1].wait_recv()

    def halo_sent(copies):
        @pl.when(s < SEQ - 1)
        def _():
            copies[0].wait_send()

        @pl.when(s > 0)
        def _():
            copies[1].wait_send()

    barrier = pltpu.get_barrier_semaphore()
    partners = [tp_dev(j) for j in range(1, 8)] + [plane_dev(j) for j in range(1, PLANE)]
    partners += [ring_dev(j) for j in range(1, NZ)] + [up, down]
    for device in partners:
        pl.semaphore_signal(barrier, inc=1, device_id=device, device_id_type=pl.DeviceIdType.MESH)

    loads = [
        pltpu.make_async_copy(src, dst, in_sem.at[i])
        for i, (src, dst) in enumerate(
            [
                (q_in, q), (k_in, k), (v_in, v), (g_in, g), (w_in, w),
                (h_in.at[pl.ds(0, FRAME)], hp.at[1, body_rows]),
                (h_in.at[pl.ds(FRAME, FRAME)], hp.at[2, body_rows]),
                (fg_in, fg),
            ]
        )
    ]
    for copy in loads:
        copy.start()
    stores = [
        pltpu.make_async_copy(src, dst, out_sem.at[i])
        for i, (src, dst) in enumerate(
            [(att_o, att_out), (ff_o, ff_out), (gq_o, gq_out), (gk_o, gk_out), (gv_o, gv_out), (gh_o, gh_out)]
        )
    ]

    blank = jnp.zeros((4, WID, CHAN), BF16)
    for buf in (hp, gp):
        buf[:, 0:WID, :] = blank
        buf[:, PAD_ROWS - WID : PAD_ROWS, :] = blank

    @pl.when(s == 0)
    def _():
        hp[0, WID : WID + FRAME, :] = jnp.zeros((FRAME, CHAN), BF16)
        gp[0, WID : WID + FRAME, :] = jnp.zeros((FRAME, CHAN), BF16)

    @pl.when(s == SEQ - 1)
    def _():
        hp[3, WID : WID + FRAME, :] = jnp.zeros((FRAME, CHAN), BF16)
        gp[3, WID : WID + FRAME, :] = jnp.zeros((FRAME, CHAN), BF16)

    row8 = lax.broadcasted_iota(jnp.int32, (8, TOK), 0)
    loads[0].wait()
    loads[1].wait()
    squares = []
    for ref in (q, k):
        vals = ref[...].astype(F32)
        squares.append(row_sums(vals * vals))
    tp1[0] = jnp.where(row8 == 0, squares[0], squares[1])

    pl.semaphore_wait(barrier, len(partners))
    round_sq = tp_round(0, tp1)
    start(round_sq)
    hidden = [hidden_halo(part) for part in range(HALO_PARTS)]
    grads = [grad_halo(part) for part in range(HALO_PARTS)]
    for copies in hidden:
        halo_start(copies)

    SPAN = 64
    cell = lax.broadcasted_iota(jnp.int32, (SPAN, HD), 0) % WID

    def tap_sum(buf, lanes, frame, row, mirror):
        sums = [None, None, None]
        for a in range(3):
            for b in range(3):
                block = buf[frame + a, pl.ds(row + b * WID, SPAN), lanes].astype(F32)
                for c in range(3):
                    tap = 9 * a + 3 * b + c
                    tap = 26 - tap if mirror else tap
                    term = w[pl.ds(tap, 1), lanes] * block
                    sums[c] = term if sums[c] is None else sums[c] + term
        left = jnp.where(cell == 0, 0.0, pltpu.roll(sums[0], 1, 0))
        right = jnp.where(cell == WID - 1, 0.0, pltpu.roll(sums[2], SPAN - 1, 0))
        return sums[1] + left + right

    TILES = HALO_COLS // HD
    SPANS = FRAME // SPAN

    def conv_step(part, store):
        def step(i, carry):
            lanes = pl.ds(pl.multiple_of(part * HALO_COLS + (i // (2 * SPANS)) * HD, HD), HD)
            store(lanes, (i // SPANS) % 2, pl.multiple_of((i % SPANS) * SPAN, SPAN))
            return carry

        lax.fori_loop(0, TILES * 2 * SPANS, step, 0)

    def forward(part):
        def store(lanes, frame, row):
            pre = tap_sum(hp, lanes, frame, row, False)
            sig = 1.0 / (1.0 + jnp.exp(-pre))
            at = pl.ds(pl.multiple_of(frame * FRAME + row, SPAN), SPAN)
            ff_o[at, lanes] = (pre * sig).astype(BF16)
            grad = fg[at, lanes].astype(F32) * sig * (1.0 + pre * (1.0 - sig))
            gp[frame + 1, pl.ds(pl.multiple_of(row + WID, WID), SPAN), lanes] = grad.astype(BF16)

        halo_arrived(hidden[part])
        conv_step(part, store)
        halo_start(grads[part])

    def backward(part):
        def store(lanes, frame, row):
            at = pl.ds(pl.multiple_of(frame * FRAME + row, SPAN), SPAN)
            gh_o[at, lanes] = tap_sum(gp, lanes, frame, row, True).astype(BF16)

        halo_arrived(grads[part])
        conv_step(part, store)

    for copy in loads[2:]:
        copy.wait()
    arrived(round_sq)
    squares = total(tp1[0], tp1, 8)
    rinv[...] = lax.rsqrt(as_columns(squares, 0, 2) * (1.0 / FEATURES) + EPS)

    z1[0] = jnp.zeros((8, HD), F32)
    gz1[0] = jnp.zeros((8, HD), F32)
    scale_k = rinv[:, HD : 2 * HD]
    for i in range(HEADS_DEV):
        feat = jnp.maximum(k[:, head(i)].astype(F32), 0.0) * scale_k
        z1[0, pl.ds(i, 1), :] = jnp.sum(feat, axis=0, keepdims=True) * (1.0 / TOKENS)
        feat = feat.astype(BF16)
        fk[:, head(i)] = feat
        kvp[head(i), :] = tn(feat, v[:, head(i)]) * (1.0 / TOKENS)
    kvs[...] = kvp[...].astype(BF16)
    round_kv1 = plane_scatter(0, kvs, kv1)
    round_z1 = plane_round(1, z1.at[0], z1)
    start(round_z1)
    start(round_kv1)

    scale_q = rinv[:, 0:HD]
    for i in range(HEADS_DEV):
        fq[:, head(i)], fql[:, head(i)] = split(jnp.maximum(q[:, head(i)].astype(F32), 0.0) * scale_q)
    forward(0)
    forward(1)

    arrived(round_z1)
    z2[0] = total(z1[0], z1, PLANE)
    round_z2 = ring_round(0, z2.at[0], z2)
    start(round_z2)
    arrived(round_kv1)
    kvc[...] = total(kvp[mine, :], kv1, PLANE)
    kv2[0] = kvc[...].astype(BF16)
    round_kv2 = ring_round(1, kv2.at[0], kv2)
    start(round_kv2)

    forward(2)
    forward(3)
    forward(4)

    arrived(round_kv2)
    kvb[mine, :] = total(kvc[...], kv2, NZ).astype(BF16)
    round_kv3 = plane_gather(2, kvb)
    start(round_kv3)

    stores[1].start()

    arrived(round_z2)
    zt[...] = total(z2[0], z2, NZ)
    for i in range(HEADS_DEV):
        feat = fq[:, head(i)]
        key_sum = jnp.broadcast_to(zt[pl.ds(i, 1), :], (HD, HD)).astype(BF16)
        inv = 1.0 / (1.0 + nt(feat, key_sum) * (1.0 / HD))
        dinv[:, head(i)] = inv
        grad, low = split(g[:, head(i)].astype(F32) * inv)
        gn[:, head(i)] = grad
        gnl[:, head(i)] = low
        gkp[head(i), :] = tn(feat, grad) * (1.0 / TOKENS)
    gks[...] = gkp[...].astype(BF16)
    round_gk1 = plane_scatter(3, gks, gk1)
    start(round_gk1)

    backward(0)

    arrived(round_kv3)
    inner = None
    for i in range(HEADS_DEV):
        feat = fq[:, head(i)]
        inv = dinv[:, head(i)]
        mat = kvb[head(i), :]
        att = (nn(feat, mat) + nn(fql[:, head(i)], mat)) * inv
        att_o[:, head(i)] = att.astype(BF16)
        prod = g[:, head(i)].astype(F32) * att * inv
        inner = prod if inner is None else inner + prod
        grad = jnp.sum(prod, axis=1, keepdims=True) * jnp.full((1, HD), -1.0 / HD, F32)
        gden[:, head(i)] = grad
        gz1[0, pl.ds(i, 1), :] = jnp.sum(grad * feat.astype(F32), axis=0, keepdims=True) * (1.0 / TOKENS)
    round_gz1 = plane_round(4, gz1.at[0], gz1)
    start(round_gz1)
    arrived(round_gk1)
    gkc[...] = total(gkp[mine, :], gk1, PLANE)
    gk2[0] = gkc[...].astype(BF16)
    round_gk2 = ring_round(2, gk2.at[0], gk2)
    start(round_gk2)
    tp2[0] = row_sums(inner)
    round_qi = tp_round(1, tp2)
    start(round_qi)
    stores[0].start()

    backward(1)

    arrived(round_gz1)
    gz2[0] = total(gz1[0], gz1, PLANE)
    round_gz2 = ring_round(3, gz2.at[0], gz2)
    start(round_gz2)

    backward(2)

    arrived(round_gk2)
    gkb[mine, :] = total(gkc[...], gk2, NZ).astype(BF16)
    round_gk3 = plane_gather(5, gkb)
    start(round_gk3)

    arrived(round_qi)
    scale_q = rinv[:, 0:HD]
    coef = as_columns(total(tp2[0], tp2, 8), 0, 1) * scale_q * scale_q * (1.0 / FEATURES)
    for i in range(HEADS_DEV):
        raw = q[:, head(i)].astype(F32)
        mat = kvb[head(i), :]
        grad = nt(gn[:, head(i)], mat) + nt(gnl[:, head(i)], mat) + gden[:, head(i)] * zt[pl.ds(i, 1), :]
        gq_o[:, head(i)] = (jnp.where(raw > 0, grad, 0.0) * scale_q - coef * raw).astype(BF16)

    stores[2].start()

    arrived(round_gz2)
    gzt[...] = total(gz2[0], gz2, NZ)
    arrived(round_gk3)
    inner = None
    for i in range(HEADS_DEV):
        feat = fk[:, head(i)]
        mat = gkb[head(i), :]
        grad = nt(v[:, head(i)], mat) + gzt[pl.ds(i, 1), :]
        gfk[:, head(i)] = grad
        prod = feat.astype(F32) * grad
        inner = prod if inner is None else inner + prod
    tp3[0] = row_sums(inner)
    round_ki = tp_round(2, tp3)
    start(round_ki)
    for i in range(HEADS_DEV):
        gv_o[:, head(i)] = nn(fk[:, head(i)], gkb[head(i), :]).astype(BF16)

    stores[4].start()

    backward(3)
    backward(4)
    stores[5].start()

    arrived(round_ki)
    scale_k = rinv[:, HD : 2 * HD]
    coef = as_columns(total(tp3[0], tp3, 8), 0, 1) * scale_k * scale_k * (1.0 / FEATURES)
    for i in range(HEADS_DEV):
        raw = k[:, head(i)].astype(F32)
        gk_o[:, head(i)] = (jnp.where(raw > 0, gfk[:, head(i)], 0.0) * scale_k - coef * raw).astype(BF16)
    stores[3].start()

    for copy in sent:
        copy.wait_send()
    for copies in hidden + grads:
        halo_sent(copies)
    for copy in stores:
        copy.wait()


def store_all(*refs):
    sem = refs[18]
    loads = [pltpu.make_async_copy(refs[i], refs[12 + i], sem.at[0, i]) for i in range(6)]
    stores = [pltpu.make_async_copy(refs[12 + i], refs[6 + i], sem.at[1, i]) for i in range(6)]
    for copy in loads:
        copy.start()
    for load, store in zip(loads, stores):
        load.wait()
        store.start()
    for copy in stores:
        copy.wait()


def body(query_act, key_act, value_act, hidden_act, conv_weight, attention_grad, feedforward_grad):
    att = jax.ShapeDtypeStruct((TOK, COLS), BF16)
    conv = jax.ShapeDtypeStruct((TOK, CHAN), BF16)

    def vmem(shape, dtype):
        return pltpu.VMEM(shape, dtype)

    def state():
        return [
            vmem((COLS, HD), F32),
            vmem((COLS, HD), BF16),
            vmem((PLANE, CHUNK, HD), BF16),
            vmem((CHUNK, HD), F32),
            vmem((NZ, CHUNK, HD), BF16),
            vmem((COLS, HD), BF16),
        ]

    narrow = lambda dtype: vmem((TOK, COLS), dtype)
    wide = lambda: vmem((TOK, CHAN), BF16)
    padded = lambda: vmem((4, PAD_ROWS, CHAN), BF16)
    dma = pltpu.SemaphoreType.DMA
    outs = pl.pallas_call(
        kernel,
        out_shape=(att, conv, att, att, att, conv),
        in_specs=[pl.BlockSpec(memory_space=pl.ANY)] * 7,
        out_specs=(pl.BlockSpec(memory_space=pl.ANY),) * 6,
        scratch_shapes=[
            narrow(BF16), narrow(BF16), narrow(BF16), narrow(BF16), wide(), vmem((27, CHAN), F32), padded(), padded(),
            narrow(BF16), wide(), narrow(BF16), narrow(BF16), narrow(BF16), wide(),
            *[narrow(BF16)] * 5, vmem((TOK, 2 * HD), F32), narrow(F32), narrow(F32), narrow(F32),
            vmem((8, 8, TOK), F32), vmem((8, 8, TOK), F32), vmem((8, 8, TOK), F32),
            *state(), *state(),
            vmem((PLANE, 8, HD), F32), vmem((NZ, 8, HD), F32), vmem((8, HD), F32),
            vmem((PLANE, 8, HD), F32), vmem((NZ, 8, HD), F32), vmem((8, HD), F32),
            dma((8,)), dma((6,)),
            dma((3, 8)), dma((3, 8)), dma((6, PLANE)), dma((6, PLANE)), dma((4, NZ)), dma((4, NZ)),
            dma((2, 2, HALO_PARTS)), dma((2, 2, HALO_PARTS)),
        ],
        compiler_params=pltpu.CompilerParams(
            collective_id=0, has_side_effects=True, vmem_limit_bytes=VMEM_LIMIT
        ),
        name="token_mixing",
    )(query_act, key_act, value_act, attention_grad, hidden_act, feedforward_grad, conv_weight)
    return pl.pallas_call(
        store_all,
        out_shape=(att, conv, att, att, att, conv),
        in_specs=[pl.BlockSpec(memory_space=pl.ANY)] * 6,
        out_specs=(pl.BlockSpec(memory_space=pl.ANY),) * 6,
        scratch_shapes=[narrow(BF16), wide(), narrow(BF16), narrow(BF16), narrow(BF16), wide(), dma((2, 6))],
        compiler_params=pltpu.CompilerParams(vmem_limit_bytes=VMEM_LIMIT),
        name="store_results",
    )(*outs)


def solution(mesh):
    in_specs = (
        P("seq", "tp"),
        P("seq", "tp"),
        P("seq", "tp"),
        P("seq", "tp"),
        P(None, "tp"),
        P("seq", "tp"),
        P("seq", "tp"),
    )
    out_specs = (P("seq", "tp"),) * 6
    return jax.shard_map(body, mesh=mesh, in_specs=in_specs, out_specs=out_specs, check_vma=False)
```

```python
import functools

import jax
import jax.numpy as jnp
from jax import lax
from jax.experimental import pallas as pl
from jax.experimental.pallas import tpu as pltpu
from jax.sharding import PartitionSpec as P

HEADS = 24
HD = 128
HGT = 8
WID = 16
EPS = 1e-06

F32 = jnp.float32
BF16 = jnp.bfloat16

TOK = 256
FRAME = HGT * WID
HEADS_DEV = 3
COLS = HEADS_DEV * HD
CHAN = 1280
PAD_ROWS = FRAME + 2 * WID
FEATURES = HEADS * HD
TOKENS = 16384

NX, NZ, NYL = 4, 8, 2
NYH, NCORE = 4, 2
PLANE = NX * NYL
CHUNK = COLS // PLANE
HALO_COLS = 256
HALO_PARTS = CHAN // HALO_COLS
SEQ = NX * NZ * NYL
VMEM_LIMIT = 58 * 1024 * 1024


def nn(a, b):
    return lax.dot_general(a, b, (((1,), (0,)), ((), ())), preferred_element_type=F32)


def nt(a, b):
    return lax.dot_general(a, b, (((1,), (1,)), ((), ())), preferred_element_type=F32)


def tn(a, b):
    return lax.dot_general(a, b, (((0,), (0,)), ((), ())), preferred_element_type=F32)


def row_sums(x):
    ones = jnp.ones((8, x.shape[1]), BF16)
    high, low = split(x)
    return nt(ones, high) + nt(ones, low)


def as_columns(rows, first, count):
    lane = lax.broadcasted_iota(jnp.int32, (8, count * HD), 1) // HD
    row = lax.broadcasted_iota(jnp.int32, (8, count * HD), 0)
    pick = jnp.where(row == lane + first, 1.0, 0.0).astype(F32)
    high = rows.astype(BF16).astype(F32)
    return tn(high, pick) + tn(rows - high, pick)


def split(x):
    high = x.astype(BF16)
    return high, (x - high.astype(F32)).astype(BF16)


def head(i):
    return pl.ds(i * HD, HD)


def kernel(
    q_in, k_in, v_in, g_in, h_in, fg_in, w_in,
    att_out, ff_out, gq_out, gk_out, gv_out, gh_out,
    q, k, v, g, fg, w, hp, gp,
    att_o, ff_o, gq_o, gk_o, gv_o, gh_o,
    fq, fql, fk, gn, gnl, qt, kt, rinv, rrow, srow, dinv, gfk,
    tp1, tp2, tp3,
    kvp, kvs, kv1, kvc, kv2, kvb,
    gkp, gks, gk1, gkc, gk2, gkb,
    z1, z2, zt, gz1, gz2, gzt,
    in_sem, out_sem,
    tp_send, tp_recv, plane_send, plane_recv, ring_send, ring_recv,
    halo_send, halo_recv,
):
    s = lax.axis_index("seq")
    t = lax.axis_index("tp")
    yl, z, x = s // (NZ * NX), (s // NX) % NZ, s % NX
    yh, core = t // NCORE, t % NCORE

    def seq_at(yl_, z_, x_):
        return (yl_ * NZ + z_) * NX + x_

    def plane_at(j):
        return (yl + j // NX) % NYL, (x + j % NX) % NX

    def plane_dev(j):
        yl_, x_ = plane_at(j)
        return {"seq": seq_at(yl_, z, x_), "tp": t}

    def ring_dev(j):
        return {"seq": seq_at(yl, (z + j) % NZ, x), "tp": t}

    def tp_dev(j):
        return {"seq": s, "tp": ((yh + j // NCORE) % NYH) * NCORE + (core + j % NCORE) % NCORE}

    def remote(src, dst, send, recv, device):
        return pltpu.make_async_remote_copy(
            src_ref=src, dst_ref=dst, send_sem=send, recv_sem=recv,
            device_id=device, device_id_type=pl.DeviceIdType.MESH,
        )

    me = yl * NX + x
    mine = pl.ds(pl.multiple_of(me * CHUNK, 16), CHUNK)

    def plane_rows(j):
        yl_, x_ = plane_at(j)
        return pl.ds(pl.multiple_of((yl_ * NX + x_) * CHUNK, 16), CHUNK)

    def tp_round(i, buf):
        return [remote(buf.at[0], buf.at[j], tp_send.at[i, j], tp_recv.at[i, j], tp_dev(j)) for j in tp_order]

    def ring_round(i, src, dst):
        return [remote(src, dst.at[j], ring_send.at[i, j], ring_recv.at[i, j], ring_dev(j)) for j in ring_order]

    def plane_round(i, src, dst):
        return [remote(src, dst.at[j], plane_send.at[i, j], plane_recv.at[i, j], plane_dev(j)) for j in plane_order]

    def plane_scatter(i, src, dst):
        return [
            remote(src.at[plane_rows(j)], dst.at[j], plane_send.at[i, j], plane_recv.at[i, j], plane_dev(j))
            for j in plane_order
        ]

    def plane_gather(i, buf):
        return [
            remote(buf.at[mine], buf.at[mine], plane_send.at[i, j], plane_recv.at[i, j], plane_dev(j))
            for j in plane_order
        ]

    tp_order = (4, 5, 2, 3, 6, 7, 1)
    ring_order = (4, 3, 5, 2, 6, 1, 7)
    plane_order = (6, 2, 5, 7, 1, 3, 4)

    sent = []

    def start(copies):
        for copy in copies:
            copy.start()
        sent.extend(copies)

    def arrived(copies):
        for copy in copies:
            copy.wait_recv()

    def total(own, buf, count):
        for j in range(1, count):
            own = own + buf[j].astype(F32)
        return own

    up = {"seq": (s + 1) % SEQ, "tp": t}
    down = {"seq": (s + SEQ - 1) % SEQ, "tp": t}
    body_rows = pl.ds(WID, FRAME)

    def halo_copies(i, part, buf, src_up, src_down):
        cols = pl.ds(part * HALO_COLS, HALO_COLS)
        to_next = remote(
            src_up(cols), buf.at[0, body_rows, cols], halo_send.at[i, 0, part], halo_recv.at[i, 0, part], up
        )
        to_prev = remote(
            src_down(cols), buf.at[3, body_rows, cols], halo_send.at[i, 1, part], halo_recv.at[i, 1, part], down
        )
        return to_next, to_prev

    def hidden_halo(part):
        return halo_copies(
            0, part, hp, lambda c: h_in.at[pl.ds(FRAME, FRAME), c], lambda c: h_in.at[pl.ds(0, FRAME), c]
        )

    def grad_halo(part):
        return halo_copies(1, part, gp, lambda c: gp.at[2, body_rows, c], lambda c: gp.at[1, body_rows, c])

    def halo_start(copies):
        @pl.when(s < SEQ - 1)
        def _():
            copies[0].start()

        @pl.when(s > 0)
        def _():
            copies[1].start()

    def halo_arrived(copies):
        @pl.when(s > 0)
        def _():
            copies[0].wait_recv()

        @pl.when(s < SEQ - 1)
        def _():
            copies[1].wait_recv()

    def halo_sent(copies):
        @pl.when(s < SEQ - 1)
        def _():
            copies[0].wait_send()

        @pl.when(s > 0)
        def _():
            copies[1].wait_send()

    loads = [
        pltpu.make_async_copy(src, dst, in_sem.at[i])
        for i, (src, dst) in enumerate(
            [
                (q_in, q), (k_in, k), (v_in, v), (g_in, g), (w_in, w),
                (h_in.at[pl.ds(0, FRAME)], hp.at[1, body_rows]),
                (h_in.at[pl.ds(FRAME, FRAME)], hp.at[2, body_rows]),
                (fg_in, fg),
            ]
        )
    ]
    for copy in loads[:2]:
        copy.start()
    barrier = pltpu.get_barrier_semaphore()
    partners = [tp_dev(j) for j in tp_order] + [plane_dev(j) for j in plane_order]
    partners += [ring_dev(j) for j in ring_order] + [up, down]
    for device in partners:
        pl.semaphore_signal(barrier, inc=1, device_id=device, device_id_type=pl.DeviceIdType.MESH)
    for copy in loads[2:]:
        copy.start()
    stores = [
        pltpu.make_async_copy(src, dst, out_sem.at[i])
        for i, (src, dst) in enumerate(
            [(att_o, att_out), (ff_o, ff_out), (gq_o, gq_out), (gk_o, gk_out), (gv_o, gv_out), (gh_o, gh_out)]
        )
    ]

    hidden = [hidden_halo(part) for part in range(HALO_PARTS)]
    grads = [grad_halo(part) for part in range(HALO_PARTS)]

    row8 = lax.broadcasted_iota(jnp.int32, (8, TOK), 0)
    loads[0].wait()
    loads[1].wait()
    squares = []
    for ref in (q, k):
        vals = [ref[:, head(i)].astype(F32) for i in range(HEADS_DEV)]
        squares.append(row_sums(vals[0] * vals[0] + vals[1] * vals[1] + vals[2] * vals[2]))
    tp1[0] = jnp.where(row8 == 0, squares[0], squares[1])
    pl.semaphore_wait(barrier, len(partners))
    round_sq = tp_round(0, tp1)
    start(round_sq)
    halo_start(hidden[0])
    halo_start(hidden[1])

    blank = jnp.zeros((4, WID, CHAN), BF16)
    for buf in (hp, gp):
        buf[:, 0:WID, :] = blank
        buf[:, PAD_ROWS - WID : PAD_ROWS, :] = blank

    @pl.when(s == 0)
    def _():
        hp[0, WID : WID + FRAME, :] = jnp.zeros((FRAME, CHAN), BF16)
        gp[0, WID : WID + FRAME, :] = jnp.zeros((FRAME, CHAN), BF16)

    @pl.when(s == SEQ - 1)
    def _():
        hp[3, WID : WID + FRAME, :] = jnp.zeros((FRAME, CHAN), BF16)
        gp[3, WID : WID + FRAME, :] = jnp.zeros((FRAME, CHAN), BF16)

    SPAN = 64
    cell = lax.broadcasted_iota(jnp.int32, (SPAN, HD), 0) % WID

    def tap_sum(buf, lanes, frame, row, mirror):
        sums = [None, None, None]
        for a in range(3):
            for b in range(3):
                block = buf[frame + a, pl.ds(row + b * WID, SPAN), lanes].astype(F32)
                for c in range(3):
                    tap = 9 * a + 3 * b + c
                    tap = 26 - tap if mirror else tap
                    term = w[pl.ds(tap, 1), lanes] * block
                    sums[c] = term if sums[c] is None else sums[c] + term
        left = jnp.where(cell == 0, 0.0, pltpu.roll(sums[0], 1, 0))
        right = jnp.where(cell == WID - 1, 0.0, pltpu.roll(sums[2], SPAN - 1, 0))
        return sums[1] + left + right

    TILES = HALO_COLS // HD
    SPANS = FRAME // SPAN

    def conv_step(part, store):
        def step(i, carry):
            lanes = pl.ds(pl.multiple_of(part * HALO_COLS + (i // (2 * SPANS)) * HD, HD), HD)
            store(lanes, (i // SPANS) % 2, pl.multiple_of((i % SPANS) * SPAN, SPAN))
            return carry

        lax.fori_loop(0, TILES * 2 * SPANS, step, 0)

    def forward(part):
        def store(lanes, frame, row):
            pre = tap_sum(hp, lanes, frame, row, False)
            sig = 1.0 / (1.0 + jnp.exp(-pre))
            at = pl.ds(pl.multiple_of(frame * FRAME + row, SPAN), SPAN)
            ff_o[at, lanes] = (pre * sig).astype(BF16)
            grad = fg[at, lanes].astype(F32) * sig * (1.0 + pre * (1.0 - sig))
            gp[frame + 1, pl.ds(pl.multiple_of(row + WID, WID), SPAN), lanes] = grad.astype(BF16)

        halo_arrived(hidden[part])
        conv_step(part, store)

    def backward(part):
        def store(lanes, frame, row):
            at = pl.ds(pl.multiple_of(frame * FRAME + row, SPAN), SPAN)
            gh_o[at, lanes] = tap_sum(gp, lanes, frame, row, True).astype(BF16)

        halo_arrived(grads[part])
        conv_step(part, store)

    for i in range(HEADS_DEV):
        kt[head(i), :] = jnp.maximum(k[:, head(i)], 0).T
        qt[head(i), :] = jnp.maximum(q[:, head(i)], 0).T
    z1[0] = jnp.zeros((8, HD), F32)
    gz1[0] = jnp.zeros((8, HD), F32)
    srow[...] = jnp.zeros((8, TOK), F32)
    for copy in loads[2:]:
        copy.wait()
    ones = jnp.ones((8, TOK), BF16)
    arrived(round_sq)
    rrow[...] = lax.rsqrt(total(tp1[0], tp1, 8) * (1.0 / FEATURES) + EPS)
    scale_k = rrow[1:2, :]
    for i in range(HEADS_DEV):
        feat, low = split(kt[head(i), :].astype(F32) * scale_k)
        z1[0, pl.ds(i, 1), :] = (nt(ones, feat) + nt(ones, low))[0:1] * (1.0 / TOKENS)
        part = nn(feat, v[:, head(i)]) * (1.0 / TOKENS)
        kvp[head(i), :] = part
        kvs[head(i), :] = part.astype(BF16)
    round_z1 = plane_round(1, z1.at[0], z1)
    start(round_z1)
    round_kv1 = plane_scatter(0, kvs, kv1)
    start(round_kv1)
    halo_start(hidden[2])

    rinv[...] = as_columns(rrow[...], 0, 2)
    scale_q = rinv[:, 0:HD]
    scale_k = rinv[:, HD : 2 * HD]
    for i in range(HEADS_DEV):
        fq[:, head(i)], fql[:, head(i)] = split(jnp.maximum(q[:, head(i)].astype(F32), 0.0) * scale_q)
        fk[:, head(i)] = (jnp.maximum(k[:, head(i)].astype(F32), 0.0) * scale_k).astype(BF16)
        qt[head(i), :] = (qt[head(i), :].astype(F32) * rrow[0:1, :]).astype(BF16)

    forward(0)
    forward(1)
    arrived(round_z1)
    z2[0] = total(z1[0], z1, PLANE)
    round_z2 = ring_round(0, z2.at[0], z2)
    start(round_z2)
    arrived(round_kv1)
    kvc[...] = total(kvp[mine, :], kv1, PLANE)
    kv2[0] = kvc[...].astype(BF16)
    round_kv2 = ring_round(1, kv2.at[0], kv2)
    start(round_kv2)
    halo_start(hidden[3])


    forward(2)
    arrived(round_z2)
    zt[...] = total(z2[0], z2, NZ)
    for i in range(HEADS_DEV):
        key_sum = jnp.broadcast_to(zt[pl.ds(i, 1), :], (HD, HD)).astype(BF16)
        inv = 1.0 / (1.0 + nt(fq[:, head(i)], key_sum) * (1.0 / HD))
        dinv[:, head(i)] = inv
        grad, low = split(g[:, head(i)].astype(F32) * inv)
        gn[:, head(i)] = grad
        gnl[:, head(i)] = low
        part = nn(qt[head(i), :], grad) * (1.0 / TOKENS)
        gkp[head(i), :] = part
        gks[head(i), :] = part.astype(BF16)
    round_gk1 = plane_scatter(3, gks, gk1)
    start(round_gk1)

    arrived(round_kv2)
    kvb[mine, :] = total(kvc[...], kv2, NZ).astype(BF16)
    round_kv3 = plane_gather(2, kvb)
    start(round_kv3)
    halo_start(hidden[4])
    forward(3)

    arrived(round_gk1)
    gkc[...] = total(gkp[mine, :], gk1, PLANE)
    gk2[0] = gkc[...].astype(BF16)
    round_gk2 = ring_round(2, gk2.at[0], gk2)
    start(round_gk2)
    halo_start(grads[0])
    halo_start(grads[1])

    arrived(round_kv3)
    for i in range(HEADS_DEV):
        mat = kvb[head(i), :]
        inv = dinv[:, head(i)]
        att = (nn(fq[:, head(i)], mat) + nn(fql[:, head(i)], mat)) * inv
        att_o[:, head(i)] = att.astype(BF16)
        inner = row_sums(g[:, head(i)].astype(F32) * inv * att)
        srow[pl.ds(i, 1), :] = inner[0:1]
        high, low = split(inner)
        feat = fq[:, head(i)]
        gz1[0, pl.ds(i, 1), :] = (nn(high, feat) + nn(low, feat))[0:1] * (-1.0 / HD / TOKENS)
    round_gz1 = plane_round(4, gz1.at[0], gz1)
    start(round_gz1)
    tp2[0] = jnp.broadcast_to(srow[0:1, :] + srow[1:2, :] + srow[2:3, :], (8, TOK))
    round_qi = tp_round(1, tp2)
    start(round_qi)
    stores[0].start()
    forward(4)
    stores[1].start()


    arrived(round_gk2)
    gkb[mine, :] = total(gkc[...], gk2, NZ).astype(BF16)
    round_gk3 = plane_gather(5, gkb)
    start(round_gk3)
    arrived(round_gz1)
    gz2[0] = total(gz1[0], gz1, PLANE)
    round_gz2 = ring_round(3, gz2.at[0], gz2)
    start(round_gz2)
    halo_start(grads[2])
    halo_start(grads[3])
    halo_start(grads[4])

    arrived(round_qi)
    scale_q = rinv[:, 0:HD]
    rowq = rrow[0:1, :]
    coef = as_columns(total(tp2[0], tp2, 8) * (rowq * rowq * (1.0 / FEATURES)), 0, 1)
    gden = as_columns(srow[...], 0, HEADS_DEV) * (-1.0 / HD)
    for i in range(HEADS_DEV):
        raw = q[:, head(i)].astype(F32)
        mat = kvb[head(i), :]
        grad = nt(gn[:, head(i)], mat) + nt(gnl[:, head(i)], mat) + gden[:, i * HD : (i + 1) * HD] * zt[pl.ds(i, 1), :]
        gq_o[:, head(i)] = (jnp.where(raw > 0, grad, 0.0) * scale_q - coef * raw).astype(BF16)
    stores[2].start()
    backward(0)

    backward(1)
    arrived(round_gk3)
    inner = None
    for i in range(HEADS_DEV):
        grad = nt(v[:, head(i)], gkb[head(i), :])
        gfk[:, head(i)] = grad
        prod = fk[:, head(i)].astype(F32) * grad
        inner = prod if inner is None else inner + prod
    inner = row_sums(inner)
    arrived(round_gz2)
    gzt[...] = total(gz2[0], gz2, NZ)
    for i in range(HEADS_DEV):
        high, low = split(jnp.broadcast_to(gzt[pl.ds(i, 1), :], (8, HD)))
        feat = fk[:, head(i)]
        inner = inner + nt(high, feat) + nt(low, feat)
    tp3[0] = inner
    round_ki = tp_round(2, tp3)
    start(round_ki)
    scale_k = rinv[:, HD : 2 * HD]
    for i in range(HEADS_DEV):
        gv_o[:, head(i)] = nn(fk[:, head(i)], gkb[head(i), :]).astype(BF16)
        grad = gfk[:, head(i)] + gzt[pl.ds(i, 1), :]
        gfk[:, head(i)] = jnp.where(k[:, head(i)].astype(F32) > 0, grad, 0.0) * scale_k
    stores[4].start()
    backward(2)
    backward(3)
    backward(4)
    stores[5].start()


    arrived(round_ki)
    rowk = rrow[1:2, :]
    coef = as_columns(total(tp3[0], tp3, 8) * (rowk * rowk * (1.0 / FEATURES)), 0, 1)
    for i in range(HEADS_DEV):
        gk_o[:, head(i)] = (gfk[:, head(i)] - coef * k[:, head(i)].astype(F32)).astype(BF16)
    stores[3].start()

    for copy in sent:
        copy.wait_send()
    for copies in hidden + grads:
        halo_sent(copies)
    for copy in stores:
        copy.wait()


def store_all(*refs):
    sem = refs[18]
    loads = [pltpu.make_async_copy(refs[i], refs[12 + i], sem.at[0, i]) for i in range(6)]
    stores = [pltpu.make_async_copy(refs[12 + i], refs[6 + i], sem.at[1, i]) for i in range(6)]
    for copy in loads:
        copy.start()
    for load, store in zip(loads, stores):
        load.wait()
        store.start()
    for copy in stores:
        copy.wait()


def body(query_act, key_act, value_act, hidden_act, conv_weight, attention_grad, feedforward_grad):
    att = jax.ShapeDtypeStruct((TOK, COLS), BF16)
    conv = jax.ShapeDtypeStruct((TOK, CHAN), BF16)

    def vmem(shape, dtype):
        return pltpu.VMEM(shape, dtype)

    def state():
        return [
            vmem((COLS, HD), F32),
            vmem((COLS, HD), BF16),
            vmem((PLANE, CHUNK, HD), BF16),
            vmem((CHUNK, HD), F32),
            vmem((NZ, CHUNK, HD), BF16),
            vmem((COLS, HD), BF16),
        ]

    narrow = lambda dtype: vmem((TOK, COLS), dtype)
    wide = lambda: vmem((TOK, CHAN), BF16)
    padded = lambda: vmem((4, PAD_ROWS, CHAN), BF16)
    dma = pltpu.SemaphoreType.DMA
    outs = pl.pallas_call(
        kernel,
        out_shape=(att, conv, att, att, att, conv),
        in_specs=[pl.BlockSpec(memory_space=pl.ANY)] * 7,
        out_specs=(pl.BlockSpec(memory_space=pl.ANY),) * 6,
        scratch_shapes=[
            narrow(BF16), narrow(BF16), narrow(BF16), narrow(BF16), wide(), vmem((27, CHAN), F32), padded(), padded(),
            narrow(BF16), wide(), narrow(BF16), narrow(BF16), narrow(BF16), wide(),
            *[narrow(BF16)] * 5, vmem((COLS, TOK), BF16), vmem((COLS, TOK), BF16),
            vmem((TOK, 2 * HD), F32), vmem((8, TOK), F32), vmem((8, TOK), F32), narrow(F32), narrow(F32),
            vmem((8, 8, TOK), F32), vmem((8, 8, TOK), F32), vmem((8, 8, TOK), F32),
            *state(), *state(),
            vmem((PLANE, 8, HD), F32), vmem((NZ, 8, HD), F32), vmem((8, HD), F32),
            vmem((PLANE, 8, HD), F32), vmem((NZ, 8, HD), F32), vmem((8, HD), F32),
            dma((8,)), dma((6,)),
            dma((3, 8)), dma((3, 8)), dma((6, PLANE)), dma((6, PLANE)), dma((4, NZ)), dma((4, NZ)),
            dma((2, 2, HALO_PARTS)), dma((2, 2, HALO_PARTS)),
        ],
        compiler_params=pltpu.CompilerParams(
            collective_id=0, has_side_effects=True, vmem_limit_bytes=VMEM_LIMIT
        ),
        name="token_mixing",
    )(query_act, key_act, value_act, attention_grad, hidden_act, feedforward_grad, conv_weight)
    return pl.pallas_call(
        store_all,
        out_shape=(att, conv, att, att, att, conv),
        in_specs=[pl.BlockSpec(memory_space=pl.ANY)] * 6,
        out_specs=(pl.BlockSpec(memory_space=pl.ANY),) * 6,
        scratch_shapes=[narrow(BF16), wide(), narrow(BF16), narrow(BF16), narrow(BF16), wide(), dma((2, 6))],
        compiler_params=pltpu.CompilerParams(vmem_limit_bytes=VMEM_LIMIT),
        name="store_results",
    )(*outs)


def solution(mesh):
    in_specs = (
        P("seq", "tp"),
        P("seq", "tp"),
        P("seq", "tp"),
        P("seq", "tp"),
        P(None, "tp"),
        P("seq", "tp"),
        P("seq", "tp"),
    )
    out_specs = (P("seq", "tp"),) * 6
    return jax.shard_map(body, mesh=mesh, in_specs=in_specs, out_specs=out_specs, check_vma=False)
```

```python
import functools

import jax
import jax.numpy as jnp
from jax import lax
from jax.experimental import pallas as pl
from jax.experimental.pallas import tpu as pltpu
from jax.sharding import PartitionSpec as P

HEADS = 24
HD = 128
HGT = 8
WID = 16
EPS = 1e-06

F32 = jnp.float32
BF16 = jnp.bfloat16

TOK = 256
FRAME = HGT * WID
HEADS_DEV = 3
COLS = HEADS_DEV * HD
CHAN = 1280
PAD_ROWS = FRAME + 2 * WID
FEATURES = HEADS * HD
TOKENS = 16384

NX, NZ, NYL = 4, 8, 2
NYH, NCORE = 4, 2
PLANE = NX * NYL
CHUNK = COLS // PLANE
HALO_COLS = 128
HALO_PARTS = CHAN // HALO_COLS
SEQ = NX * NZ * NYL
SENT_EARLY = 8
VMEM_LIMIT = 58 * 1024 * 1024


def nn(a, b):
    return lax.dot_general(a, b, (((1,), (0,)), ((), ())), preferred_element_type=F32)


def nt(a, b):
    return lax.dot_general(a, b, (((1,), (1,)), ((), ())), preferred_element_type=F32)


def tn(a, b):
    return lax.dot_general(a, b, (((0,), (0,)), ((), ())), preferred_element_type=F32)


def row_sums(x):
    ones = jnp.ones((8, x.shape[1]), BF16)
    high, low = split(x)
    return nt(ones, high) + nt(ones, low)


def as_columns(rows, first, count):
    lane = lax.broadcasted_iota(jnp.int32, (8, count * HD), 1) // HD
    row = lax.broadcasted_iota(jnp.int32, (8, count * HD), 0)
    pick = jnp.where(row == lane + first, 1.0, 0.0).astype(F32)
    high = rows.astype(BF16).astype(F32)
    return tn(high, pick) + tn(rows - high, pick)


def split(x):
    high = x.astype(BF16)
    return high, (x - high.astype(F32)).astype(BF16)


def head(i):
    return pl.ds(i * HD, HD)


def kernel(
    q_in, k_in, v_in, g_in, h_in, fg_in, w_in,
    att_out, ff_out, gq_out, gk_out, gv_out, gh_out,
    q, k, v, g, fg, w, hp, gp,
    att_o, ff_o, gq_o, gk_o, gv_o, gh_o,
    fq, fql, fk, gn, gnl, qt, kt, rinv, rrow, srow, dinv, gfk,
    tp1, tp2, tp3,
    kvp, kvs, kv1, kvc, kv2, kvb,
    gkp, gks, gk1, gkc, gk2, gkb,
    z1, z2, zt, gz1, gz2, gzt,
    in_sem, out_sem,
    tp_send, tp_recv, plane_send, plane_recv, ring_send, ring_recv,
    halo_send, halo_recv,
):
    s = lax.axis_index("seq")
    t = lax.axis_index("tp")
    yl, z, x = s // (NZ * NX), (s // NX) % NZ, s % NX
    yh, core = t // NCORE, t % NCORE

    def seq_at(yl_, z_, x_):
        return (yl_ * NZ + z_) * NX + x_

    def plane_at(j):
        return (yl + j // NX) % NYL, (x + j % NX) % NX

    def plane_dev(j):
        yl_, x_ = plane_at(j)
        return {"seq": seq_at(yl_, z, x_), "tp": t}

    def ring_dev(j):
        return {"seq": seq_at(yl, (z + j) % NZ, x), "tp": t}

    def tp_dev(j):
        return {"seq": s, "tp": ((yh + j // NCORE) % NYH) * NCORE + (core + j % NCORE) % NCORE}

    def remote(src, dst, send, recv, device):
        return pltpu.make_async_remote_copy(
            src_ref=src, dst_ref=dst, send_sem=send, recv_sem=recv,
            device_id=device, device_id_type=pl.DeviceIdType.MESH,
        )

    me = yl * NX + x
    mine = pl.ds(pl.multiple_of(me * CHUNK, 16), CHUNK)

    def plane_rows(j):
        yl_, x_ = plane_at(j)
        return pl.ds(pl.multiple_of((yl_ * NX + x_) * CHUNK, 16), CHUNK)

    def exchange(copies, whole, send, recv):
        return copies, pltpu.make_async_copy(whole, whole, send), pltpu.make_async_copy(whole, whole, recv)

    tp_order = (4, 5, 2, 3, 6, 7, 1)
    ring_order = (4, 3, 5, 2, 6, 1, 7)
    plane_order = (6, 2, 5, 7, 1, 3, 4)
    others = pl.ds(1, 7)

    def tp_round(i, buf):
        sems = tp_send.at[i], tp_recv.at[i]
        return exchange([remote(buf.at[0], buf.at[j], *sems, tp_dev(j)) for j in tp_order], buf.at[others], *sems)

    def ring_round(i, src, dst):
        sems = ring_send.at[i], ring_recv.at[i]
        return exchange([remote(src, dst.at[j], *sems, ring_dev(j)) for j in ring_order], dst.at[others], *sems)

    def plane_round(i, src, dst):
        sems = plane_send.at[i], plane_recv.at[i]
        return exchange([remote(src, dst.at[j], *sems, plane_dev(j)) for j in plane_order], dst.at[others], *sems)

    def plane_scatter(i, src, dst):
        sems = plane_send.at[i], plane_recv.at[i]
        copies = [remote(src.at[plane_rows(j)], dst.at[j], *sems, plane_dev(j)) for j in plane_order]
        return exchange(copies, dst.at[others], *sems)

    def plane_gather(i, buf):
        sems = plane_send.at[i], plane_recv.at[i]
        copies = [remote(buf.at[mine], buf.at[mine], *sems, plane_dev(j)) for j in plane_order]
        return exchange(copies, buf.at[pl.ds(0, (PLANE - 1) * CHUNK)], *sems)

    sent = []

    def start(round_):
        for copy in round_[0]:
            copy.start()
        sent.append(round_[1])

    def arrived(round_):
        round_[2].wait()

    def total(own, buf, count):
        for j in range(1, count):
            own = own + buf[j].astype(F32)
        return own

    up = {"seq": (s + 1) % SEQ, "tp": t}
    down = {"seq": (s + SEQ - 1) % SEQ, "tp": t}
    body_rows = pl.ds(WID, FRAME)

    def halo_copies(i, part, buf, src_up, src_down):
        cols = pl.ds(part * HALO_COLS, HALO_COLS)
        to_next = remote(
            src_up(cols), buf.at[0, body_rows, cols], halo_send.at[i, 0], halo_recv.at[i, 0, part], up
        )
        to_prev = remote(
            src_down(cols), buf.at[3, body_rows, cols], halo_send.at[i, 1], halo_recv.at[i, 1, part], down
        )
        return to_next, to_prev

    def hidden_halo(part):
        return halo_copies(
            0, part, hp, lambda c: h_in.at[pl.ds(FRAME, FRAME), c], lambda c: h_in.at[pl.ds(0, FRAME), c]
        )

    def grad_halo(part):
        return halo_copies(1, part, gp, lambda c: gp.at[2, body_rows, c], lambda c: gp.at[1, body_rows, c])

    def halo_start(copies):
        @pl.when(s < SEQ - 1)
        def _():
            copies[0].start()

        @pl.when(s > 0)
        def _():
            copies[1].start()

    def halo_arrived(copies):
        @pl.when(s > 0)
        def _():
            copies[0].wait_recv()

        @pl.when(s < SEQ - 1)
        def _():
            copies[1].wait_recv()

    def halo_sent(i, buf):
        frame = buf.at[0, body_rows]

        @pl.when(s < SEQ - 1)
        def _():
            pltpu.make_async_copy(frame, frame, halo_send.at[i, 0]).wait()

        @pl.when(s > 0)
        def _():
            pltpu.make_async_copy(frame, frame, halo_send.at[i, 1]).wait()

    loads = [
        pltpu.make_async_copy(src, dst, in_sem.at[i])
        for i, (src, dst) in enumerate(
            [
                (q_in, q), (k_in, k), (v_in, v), (g_in, g), (w_in, w),
                (h_in.at[pl.ds(0, FRAME)], hp.at[1, body_rows]),
                (h_in.at[pl.ds(FRAME, FRAME)], hp.at[2, body_rows]),
                (fg_in, fg),
            ]
        )
    ]
    for copy in loads[:2]:
        copy.start()
    barrier = pltpu.get_barrier_semaphore()
    partners = [tp_dev(j) for j in tp_order] + [plane_dev(j) for j in plane_order]
    partners += [ring_dev(j) for j in ring_order] + [up, down]
    for device in partners:
        pl.semaphore_signal(barrier, inc=1, device_id=device, device_id_type=pl.DeviceIdType.MESH)
    for copy in loads[2:]:
        copy.start()
    stores = [
        pltpu.make_async_copy(src, dst, out_sem.at[i])
        for i, (src, dst) in enumerate(
            [(att_o, att_out), (ff_o, ff_out), (gq_o, gq_out), (gk_o, gk_out), (gv_o, gv_out), (gh_o, gh_out)]
        )
    ]

    hidden = [hidden_halo(part) for part in range(HALO_PARTS)]
    grads = [grad_halo(part) for part in range(HALO_PARTS)]

    row8 = lax.broadcasted_iota(jnp.int32, (8, TOK), 0)
    loads[0].wait()
    loads[1].wait()
    squares = []
    for ref in (q, k):
        vals = [ref[:, head(i)].astype(F32) for i in range(HEADS_DEV)]
        squares.append(row_sums(vals[0] * vals[0] + vals[1] * vals[1] + vals[2] * vals[2]))
    tp1[0] = jnp.where(row8 == 0, squares[0], squares[1])
    pl.semaphore_wait(barrier, len(partners))
    round_sq = tp_round(0, tp1)
    start(round_sq)
    halo_start(hidden[0])
    halo_start(hidden[1])
    halo_start(hidden[2])
    halo_start(hidden[3])

    blank = jnp.zeros((4, WID, CHAN), BF16)
    for buf in (hp, gp):
        buf[:, 0:WID, :] = blank
        buf[:, PAD_ROWS - WID : PAD_ROWS, :] = blank

    @pl.when(s == 0)
    def _():
        hp[0, WID : WID + FRAME, :] = jnp.zeros((FRAME, CHAN), BF16)
        gp[0, WID : WID + FRAME, :] = jnp.zeros((FRAME, CHAN), BF16)

    @pl.when(s == SEQ - 1)
    def _():
        hp[3, WID : WID + FRAME, :] = jnp.zeros((FRAME, CHAN), BF16)
        gp[3, WID : WID + FRAME, :] = jnp.zeros((FRAME, CHAN), BF16)

    SPAN = 64
    cell = lax.broadcasted_iota(jnp.int32, (SPAN, HD), 0) % WID

    def tap_sum(buf, lanes, frame, row, mirror):
        sums = [None, None, None]
        for a in range(3):
            for b in range(3):
                block = buf[frame + a, pl.ds(row + b * WID, SPAN), lanes].astype(F32)
                for c in range(3):
                    tap = 9 * a + 3 * b + c
                    tap = 26 - tap if mirror else tap
                    term = w[pl.ds(tap, 1), lanes] * block
                    sums[c] = term if sums[c] is None else sums[c] + term
        left = jnp.where(cell == 0, 0.0, pltpu.roll(sums[0], 1, 0))
        right = jnp.where(cell == WID - 1, 0.0, pltpu.roll(sums[2], SPAN - 1, 0))
        return sums[1] + left + right

    TILES = HALO_COLS // HD
    SPANS = FRAME // SPAN

    def conv_step(part, store):
        def step(i, carry):
            lanes = pl.ds(pl.multiple_of(part * HALO_COLS + (i // (2 * SPANS)) * HD, HD), HD)
            store(lanes, (i // SPANS) % 2, pl.multiple_of((i % SPANS) * SPAN, SPAN))
            return carry

        lax.fori_loop(0, TILES * 2 * SPANS, step, 0)

    def forward(part):
        def store(lanes, frame, row):
            pre = tap_sum(hp, lanes, frame, row, False)
            sig = 1.0 / (1.0 + jnp.exp(-pre))
            at = pl.ds(pl.multiple_of(frame * FRAME + row, SPAN), SPAN)
            ff_o[at, lanes] = (pre * sig).astype(BF16)
            grad = fg[at, lanes].astype(F32) * sig * (1.0 + pre * (1.0 - sig))
            gp[frame + 1, pl.ds(pl.multiple_of(row + WID, WID), SPAN), lanes] = grad.astype(BF16)

        halo_arrived(hidden[part])
        conv_step(part, store)

    def backward(part):
        def store(lanes, frame, row):
            at = pl.ds(pl.multiple_of(frame * FRAME + row, SPAN), SPAN)
            gh_o[at, lanes] = tap_sum(gp, lanes, frame, row, True).astype(BF16)

        halo_arrived(grads[part])
        conv_step(part, store)

    for i in range(HEADS_DEV):
        kt[head(i), :] = jnp.maximum(k[:, head(i)], 0).T
        qt[head(i), :] = jnp.maximum(q[:, head(i)], 0).T
    z1[0] = jnp.zeros((8, HD), F32)
    gz1[0] = jnp.zeros((8, HD), F32)
    srow[...] = jnp.zeros((8, TOK), F32)
    for copy in loads[2:]:
        copy.wait()
    ones = jnp.ones((8, TOK), BF16)
    arrived(round_sq)
    rrow[...] = lax.rsqrt(total(tp1[0], tp1, 8) * (1.0 / FEATURES) + EPS)
    scale_k = rrow[1:2, :]
    for i in range(HEADS_DEV):
        feat = (kt[head(i), :].astype(F32) * scale_k).astype(BF16)
        z1[0, pl.ds(i, 1), :] = nt(ones, feat)[0:1] * (1.0 / TOKENS)
        part = nn(feat, v[:, head(i)]) * (1.0 / TOKENS)
        kvp[head(i), :] = part
        kvs[head(i), :] = part.astype(BF16)
    round_z1 = plane_round(1, z1.at[0], z1)
    start(round_z1)
    round_kv1 = plane_scatter(0, kvs, kv1)
    start(round_kv1)

    rinv[...] = as_columns(rrow[...], 0, 2)
    scale_q = rinv[:, 0:HD]
    scale_k = rinv[:, HD : 2 * HD]
    for i in range(HEADS_DEV):
        fq[:, head(i)], fql[:, head(i)] = split(jnp.maximum(q[:, head(i)].astype(F32), 0.0) * scale_q)
        fk[:, head(i)] = (jnp.maximum(k[:, head(i)].astype(F32), 0.0) * scale_k).astype(BF16)
        qt[head(i), :] = (qt[head(i), :].astype(F32) * rrow[0:1, :]).astype(BF16)

    halo_start(hidden[4])
    forward(0)
    forward(1)
    forward(2)
    halo_start(hidden[5])
    arrived(round_z1)
    z2[0] = total(z1[0], z1, PLANE)
    round_z2 = ring_round(0, z2.at[0], z2)
    start(round_z2)
    arrived(round_kv1)
    kvc[...] = total(kvp[mine, :], kv1, PLANE)
    kv2[0] = kvc[...].astype(BF16)
    round_kv2 = ring_round(1, kv2.at[0], kv2)
    start(round_kv2)
    halo_start(hidden[6])


    forward(3)
    forward(4)
    halo_start(hidden[7])
    arrived(round_z2)
    zt[...] = total(z2[0], z2, NZ)
    for i in range(HEADS_DEV):
        key_sum = jnp.broadcast_to(zt[pl.ds(i, 1), :], (HD, HD)).astype(BF16)
        inv = 1.0 / (1.0 + nt(fq[:, head(i)], key_sum) * (1.0 / HD))
        dinv[:, head(i)] = inv
        grad, low = split(g[:, head(i)].astype(F32) * inv)
        gn[:, head(i)] = grad
        gnl[:, head(i)] = low
        part = nn(qt[head(i), :], grad) * (1.0 / TOKENS)
        gkp[head(i), :] = part
        gks[head(i), :] = part.astype(BF16)
    round_gk1 = plane_scatter(3, gks, gk1)
    start(round_gk1)

    arrived(round_kv2)
    kvb[mine, :] = total(kvc[...], kv2, NZ).astype(BF16)
    round_kv3 = plane_gather(2, kvb)
    start(round_kv3)
    halo_start(hidden[8])
    forward(5)
    halo_start(hidden[9])
    forward(6)

    arrived(round_gk1)
    gkc[...] = total(gkp[mine, :], gk1, PLANE)
    gk2[0] = gkc[...].astype(BF16)
    round_gk2 = ring_round(2, gk2.at[0], gk2)
    start(round_gk2)

    arrived(round_kv3)
    for i in range(HEADS_DEV):
        mat = kvb[head(i), :]
        inv = dinv[:, head(i)]
        att = (nn(fq[:, head(i)], mat) + nn(fql[:, head(i)], mat)) * inv
        att_o[:, head(i)] = att.astype(BF16)
        inner = row_sums(g[:, head(i)].astype(F32) * inv * att)
        srow[pl.ds(i, 1), :] = inner[0:1]
        high, low = split(inner)
        feat = fq[:, head(i)]
        gz1[0, pl.ds(i, 1), :] = (nn(high, feat) + nn(low, feat))[0:1] * (-1.0 / HD / TOKENS)
    round_gz1 = plane_round(4, gz1.at[0], gz1)
    start(round_gz1)
    tp2[0] = jnp.broadcast_to(srow[0:1, :] + srow[1:2, :] + srow[2:3, :], (8, TOK))
    round_qi = tp_round(1, tp2)
    start(round_qi)
    stores[0].start()
    halo_start(grads[0])
    halo_start(grads[1])
    forward(7)
    forward(8)
    halo_start(grads[2])


    arrived(round_gk2)
    gkb[mine, :] = total(gkc[...], gk2, NZ).astype(BF16)
    round_gk3 = plane_gather(5, gkb)
    start(round_gk3)
    arrived(round_gz1)
    gz2[0] = total(gz1[0], gz1, PLANE)
    round_gz2 = ring_round(3, gz2.at[0], gz2)
    start(round_gz2)
    halo_start(grads[3])
    halo_start(grads[4])
    forward(9)
    stores[1].start()

    arrived(round_qi)
    scale_q = rinv[:, 0:HD]
    rowq = rrow[0:1, :]
    coef = as_columns(total(tp2[0], tp2, 8) * (rowq * rowq * (1.0 / FEATURES)), 0, 1)
    gden = as_columns(srow[...], 0, HEADS_DEV) * (-1.0 / HD)
    for i in range(HEADS_DEV):
        raw = q[:, head(i)].astype(F32)
        mat = kvb[head(i), :]
        grad = nt(gn[:, head(i)], mat) + nt(gnl[:, head(i)], mat) + gden[:, i * HD : (i + 1) * HD] * zt[pl.ds(i, 1), :]
        gq_o[:, head(i)] = (jnp.where(raw > 0, grad, 0.0) * scale_q - coef * raw).astype(BF16)
    stores[2].start()
    backward(0)
    halo_start(grads[5])
    backward(1)
    halo_start(grads[6])
    backward(2)

    for copy in sent[:SENT_EARLY]:
        copy.wait()
    halo_sent(0, hp)

    arrived(round_gk3)
    inner = None
    for i in range(HEADS_DEV):
        grad = nt(v[:, head(i)], gkb[head(i), :])
        gfk[:, head(i)] = grad
        prod = fk[:, head(i)].astype(F32) * grad
        inner = prod if inner is None else inner + prod
    inner = row_sums(inner)
    arrived(round_gz2)
    gzt[...] = total(gz2[0], gz2, NZ)
    for i in range(HEADS_DEV):
        high, low = split(jnp.broadcast_to(gzt[pl.ds(i, 1), :], (8, HD)))
        feat = fk[:, head(i)]
        inner = inner + nt(high, feat) + nt(low, feat)
    tp3[0] = inner
    round_ki = tp_round(2, tp3)
    start(round_ki)
    halo_start(grads[7])
    halo_start(grads[8])
    halo_start(grads[9])
    scale_k = rinv[:, HD : 2 * HD]
    for i in range(HEADS_DEV):
        gv_o[:, head(i)] = nn(fk[:, head(i)], gkb[head(i), :]).astype(BF16)
        grad = gfk[:, head(i)] + gzt[pl.ds(i, 1), :]
        gfk[:, head(i)] = jnp.where(k[:, head(i)].astype(F32) > 0, grad, 0.0) * scale_k
    stores[4].start()
    backward(3)
    backward(4)
    backward(5)
    backward(6)
    backward(7)
    backward(8)
    backward(9)
    stores[5].start()


    arrived(round_ki)
    rowk = rrow[1:2, :]
    coef = as_columns(total(tp3[0], tp3, 8) * (rowk * rowk * (1.0 / FEATURES)), 0, 1)
    for i in range(HEADS_DEV):
        gk_o[:, head(i)] = (gfk[:, head(i)] - coef * k[:, head(i)].astype(F32)).astype(BF16)
    stores[3].start()

    for copy in sent[SENT_EARLY:]:
        copy.wait()
    halo_sent(1, gp)
    for copy in stores:
        copy.wait()


def store_all(*refs):
    sem = refs[18]
    loads = [pltpu.make_async_copy(refs[i], refs[12 + i], sem.at[0, i]) for i in range(6)]
    stores = [pltpu.make_async_copy(refs[12 + i], refs[6 + i], sem.at[1, i]) for i in range(6)]
    for copy in loads:
        copy.start()
    for load, store in zip(loads, stores):
        load.wait()
        store.start()
    for copy in stores:
        copy.wait()


def body(query_act, key_act, value_act, hidden_act, conv_weight, attention_grad, feedforward_grad):
    att = jax.ShapeDtypeStruct((TOK, COLS), BF16)
    conv = jax.ShapeDtypeStruct((TOK, CHAN), BF16)

    def vmem(shape, dtype):
        return pltpu.VMEM(shape, dtype)

    def state():
        return [
            vmem((COLS, HD), F32),
            vmem((COLS, HD), BF16),
            vmem((PLANE, CHUNK, HD), BF16),
            vmem((CHUNK, HD), F32),
            vmem((NZ, CHUNK, HD), BF16),
            vmem((COLS, HD), BF16),
        ]

    narrow = lambda dtype: vmem((TOK, COLS), dtype)
    wide = lambda: vmem((TOK, CHAN), BF16)
    padded = lambda: vmem((4, PAD_ROWS, CHAN), BF16)
    dma = pltpu.SemaphoreType.DMA
    outs = pl.pallas_call(
        kernel,
        out_shape=(att, conv, att, att, att, conv),
        in_specs=[pl.BlockSpec(memory_space=pl.ANY)] * 7,
        out_specs=(pl.BlockSpec(memory_space=pl.ANY),) * 6,
        scratch_shapes=[
            narrow(BF16), narrow(BF16), narrow(BF16), narrow(BF16), wide(), vmem((27, CHAN), F32), padded(), padded(),
            narrow(BF16), wide(), narrow(BF16), narrow(BF16), narrow(BF16), wide(),
            *[narrow(BF16)] * 5, vmem((COLS, TOK), BF16), vmem((COLS, TOK), BF16),
            vmem((TOK, 2 * HD), F32), vmem((8, TOK), F32), vmem((8, TOK), F32), narrow(F32), narrow(F32),
            vmem((8, 8, TOK), F32), vmem((8, 8, TOK), F32), vmem((8, 8, TOK), F32),
            *state(), *state(),
            vmem((PLANE, 8, HD), F32), vmem((NZ, 8, HD), F32), vmem((8, HD), F32),
            vmem((PLANE, 8, HD), F32), vmem((NZ, 8, HD), F32), vmem((8, HD), F32),
            dma((8,)), dma((6,)),
            dma((3,)), dma((3,)), dma((6,)), dma((6,)), dma((4,)), dma((4,)),
            dma((2, 2)), dma((2, 2, HALO_PARTS)),
        ],
        compiler_params=pltpu.CompilerParams(
            collective_id=0, has_side_effects=True, vmem_limit_bytes=VMEM_LIMIT
        ),
        name="token_mixing",
    )(query_act, key_act, value_act, attention_grad, hidden_act, feedforward_grad, conv_weight)
    return pl.pallas_call(
        store_all,
        out_shape=(att, conv, att, att, att, conv),
        in_specs=[pl.BlockSpec(memory_space=pl.ANY)] * 6,
        out_specs=(pl.BlockSpec(memory_space=pl.ANY),) * 6,
        scratch_shapes=[narrow(BF16), wide(), narrow(BF16), narrow(BF16), narrow(BF16), wide(), dma((2, 6))],
        compiler_params=pltpu.CompilerParams(vmem_limit_bytes=VMEM_LIMIT),
        name="store_results",
    )(*outs)


def solution(mesh):
    in_specs = (
        P("seq", "tp"),
        P("seq", "tp"),
        P("seq", "tp"),
        P("seq", "tp"),
        P(None, "tp"),
        P("seq", "tp"),
        P("seq", "tp"),
    )
    out_specs = (P("seq", "tp"),) * 6
    return jax.shard_map(body, mesh=mesh, in_specs=in_specs, out_specs=out_specs, check_vma=False)
```

```python
import functools

import jax
import jax.numpy as jnp
from jax import lax
from jax.experimental import pallas as pl
from jax.experimental.pallas import tpu as pltpu
from jax.sharding import PartitionSpec as P

HEADS = 24
HD = 128
HGT = 8
WID = 16
EPS = 1e-06

F32 = jnp.float32
BF16 = jnp.bfloat16

TOK = 256
FRAME = HGT * WID
HEADS_DEV = 3
COLS = HEADS_DEV * HD
CHAN = 1280
PAD_ROWS = FRAME + 2 * WID
FEATURES = HEADS * HD
TOKENS = 16384

NX, NZ, NYL = 4, 8, 2
NYH, NCORE = 4, 2
PLANE = NX * NYL
CHUNK = COLS // PLANE
HALO_COLS = 128
HALO_PARTS = CHAN // HALO_COLS
SEQ = NX * NZ * NYL
SENT_EARLY = 8
VMEM_LIMIT = 58 * 1024 * 1024


def nn(a, b):
    return lax.dot_general(a, b, (((1,), (0,)), ((), ())), preferred_element_type=F32)


def nt(a, b):
    return lax.dot_general(a, b, (((1,), (1,)), ((), ())), preferred_element_type=F32)


def tn(a, b):
    return lax.dot_general(a, b, (((0,), (0,)), ((), ())), preferred_element_type=F32)


def row_sums(x):
    ones = jnp.ones((8, x.shape[1]), BF16)
    high, low = split(x)
    return nt(ones, high) + nt(ones, low)


def as_columns(rows, first, count):
    lane = lax.broadcasted_iota(jnp.int32, (8, count * HD), 1) // HD
    row = lax.broadcasted_iota(jnp.int32, (8, count * HD), 0)
    pick = jnp.where(row == lane + first, 1.0, 0.0).astype(F32)
    high = rows.astype(BF16).astype(F32)
    return tn(high, pick) + tn(rows - high, pick)


def split(x):
    high = x.astype(BF16)
    return high, (x - high.astype(F32)).astype(BF16)


def head(i):
    return pl.ds(i * HD, HD)


def kernel(
    q_in, k_in, v_in, g_in, h_in, fg_in, w_in,
    att_out, ff_out, gq_out, gk_out, gv_out, gh_out,
    q, k, v, g, fg, w, hp, gp,
    att_o, ff_o, gq_o, gk_o, gv_o, gh_o,
    fq, fql, fk, gn, gnl, qt, kt, rinv, rrow, srow, dinv, gfk,
    tp1, tp2, tp3,
    kvp, kvs, kv1, kvc, kv2, kvb,
    gkp, gks, gk1, gkc, gk2, gkb,
    z1, z2, zt, gz1, gz2, gzt,
    in_sem, out_sem,
    tp_send, tp_recv, plane_send, plane_recv, ring_send, ring_recv,
    halo_send, halo_recv,
):
    s = lax.axis_index("seq")
    t = lax.axis_index("tp")
    yl, z, x = s // (NZ * NX), (s // NX) % NZ, s % NX
    yh, core = t // NCORE, t % NCORE

    def seq_at(yl_, z_, x_):
        return (yl_ * NZ + z_) * NX + x_

    def plane_at(j):
        return (yl + j // NX) % NYL, (x + j % NX) % NX

    def plane_dev(j):
        yl_, x_ = plane_at(j)
        return {"seq": seq_at(yl_, z, x_), "tp": t}

    def ring_dev(j):
        return {"seq": seq_at(yl, (z + j) % NZ, x), "tp": t}

    def tp_dev(j):
        return {"seq": s, "tp": ((yh + j // NCORE) % NYH) * NCORE + (core + j % NCORE) % NCORE}

    def remote(src, dst, send, recv, device):
        return pltpu.make_async_remote_copy(
            src_ref=src, dst_ref=dst, send_sem=send, recv_sem=recv,
            device_id=device, device_id_type=pl.DeviceIdType.MESH,
        )

    me = yl * NX + x
    mine = pl.ds(pl.multiple_of(me * CHUNK, 16), CHUNK)

    def plane_rows(j):
        yl_, x_ = plane_at(j)
        return pl.ds(pl.multiple_of((yl_ * NX + x_) * CHUNK, 16), CHUNK)

    def exchange(copies, whole, send, recv):
        return copies, pltpu.make_async_copy(whole, whole, send), pltpu.make_async_copy(whole, whole, recv)

    tp_order = (4, 5, 2, 3, 6, 7, 1)
    ring_order = (4, 3, 5, 2, 6, 1, 7)
    plane_order = (6, 2, 5, 7, 1, 3, 4)
    others = pl.ds(1, 7)

    def tp_round(i, buf):
        sems = tp_send.at[i], tp_recv.at[i]
        return exchange([remote(buf.at[0], buf.at[j], *sems, tp_dev(j)) for j in tp_order], buf.at[others], *sems)

    def ring_round(i, src, dst):
        sems = ring_send.at[i], ring_recv.at[i]
        return exchange([remote(src, dst.at[j], *sems, ring_dev(j)) for j in ring_order], dst.at[others], *sems)

    def plane_round(i, src, dst):
        sems = plane_send.at[i], plane_recv.at[i]
        return exchange([remote(src, dst.at[j], *sems, plane_dev(j)) for j in plane_order], dst.at[others], *sems)

    def plane_scatter(i, src, dst):
        sems = plane_send.at[i], plane_recv.at[i]
        copies = [remote(src.at[plane_rows(j)], dst.at[j], *sems, plane_dev(j)) for j in plane_order]
        return exchange(copies, dst.at[others], *sems)

    def plane_gather(i, buf):
        sems = plane_send.at[i], plane_recv.at[i]
        copies = [remote(buf.at[mine], buf.at[mine], *sems, plane_dev(j)) for j in plane_order]
        return exchange(copies, buf.at[pl.ds(0, (PLANE - 1) * CHUNK)], *sems)

    sent = []

    def start(round_):
        for copy in round_[0]:
            copy.start()
        sent.append(round_[1])

    def arrived(round_):
        round_[2].wait()

    def total(own, buf, count):
        for j in range(1, count):
            own = own + buf[j].astype(F32)
        return own

    up = {"seq": (s + 1) % SEQ, "tp": t}
    down = {"seq": (s + SEQ - 1) % SEQ, "tp": t}
    body_rows = pl.ds(WID, FRAME)

    def halo_copies(i, part, buf, src_up, src_down):
        cols = pl.ds(part * HALO_COLS, HALO_COLS)
        to_next = remote(
            src_up(cols), buf.at[0, body_rows, cols], halo_send.at[i, 0], halo_recv.at[i, 0, part], up
        )
        to_prev = remote(
            src_down(cols), buf.at[3, body_rows, cols], halo_send.at[i, 1], halo_recv.at[i, 1, part], down
        )
        return to_next, to_prev

    def hidden_halo(part):
        return halo_copies(
            0, part, hp, lambda c: h_in.at[pl.ds(FRAME, FRAME), c], lambda c: h_in.at[pl.ds(0, FRAME), c]
        )

    def grad_halo(part):
        return halo_copies(1, part, gp, lambda c: gp.at[2, body_rows, c], lambda c: gp.at[1, body_rows, c])

    def halo_start(copies):
        @pl.when(s < SEQ - 1)
        def _():
            copies[0].start()

        @pl.when(s > 0)
        def _():
            copies[1].start()

    def halo_arrived(copies):
        @pl.when(s > 0)
        def _():
            copies[0].wait_recv()

        @pl.when(s < SEQ - 1)
        def _():
            copies[1].wait_recv()

    def halo_sent(i, buf):
        frame = buf.at[0, body_rows]

        @pl.when(s < SEQ - 1)
        def _():
            pltpu.make_async_copy(frame, frame, halo_send.at[i, 0]).wait()

        @pl.when(s > 0)
        def _():
            pltpu.make_async_copy(frame, frame, halo_send.at[i, 1]).wait()

    loads = [
        pltpu.make_async_copy(src, dst, in_sem.at[i])
        for i, (src, dst) in enumerate(
            [
                (q_in, q), (k_in, k), (v_in, v), (g_in, g), (w_in, w),
                (h_in.at[pl.ds(0, FRAME)], hp.at[1, body_rows]),
                (h_in.at[pl.ds(FRAME, FRAME)], hp.at[2, body_rows]),
                (fg_in, fg),
            ]
        )
    ]
    for copy in loads[:2]:
        copy.start()
    barrier = pltpu.get_barrier_semaphore()
    partners = [tp_dev(j) for j in tp_order] + [plane_dev(j) for j in plane_order]
    partners += [ring_dev(j) for j in ring_order] + [up, down]
    for device in partners:
        pl.semaphore_signal(barrier, inc=1, device_id=device, device_id_type=pl.DeviceIdType.MESH)
    for copy in loads[2:]:
        copy.start()
    stores = [
        pltpu.make_async_copy(src, dst, out_sem.at[i])
        for i, (src, dst) in enumerate(
            [(att_o, att_out), (ff_o, ff_out), (gq_o, gq_out), (gk_o, gk_out), (gv_o, gv_out), (gh_o, gh_out)]
        )
    ]

    hidden = [hidden_halo(part) for part in range(HALO_PARTS)]
    grads = [grad_halo(part) for part in range(HALO_PARTS)]

    row8 = lax.broadcasted_iota(jnp.int32, (8, TOK), 0)
    loads[0].wait()
    loads[1].wait()
    squares = []
    for ref in (q, k):
        vals = [ref[:, head(i)].astype(F32) for i in range(HEADS_DEV)]
        squares.append(row_sums(vals[0] * vals[0] + vals[1] * vals[1] + vals[2] * vals[2]))
    tp1[0] = jnp.where(row8 == 0, squares[0], squares[1])
    pl.semaphore_wait(barrier, len(partners))
    round_sq = tp_round(0, tp1)
    start(round_sq)
    halo_start(hidden[0])
    halo_start(hidden[1])
    halo_start(hidden[2])
    halo_start(hidden[3])

    blank = jnp.zeros((4, WID, CHAN), BF16)
    for buf in (hp, gp):
        buf[:, 0:WID, :] = blank
        buf[:, PAD_ROWS - WID : PAD_ROWS, :] = blank

    @pl.when(s == 0)
    def _():
        hp[0, WID : WID + FRAME, :] = jnp.zeros((FRAME, CHAN), BF16)
        gp[0, WID : WID + FRAME, :] = jnp.zeros((FRAME, CHAN), BF16)

    @pl.when(s == SEQ - 1)
    def _():
        hp[3, WID : WID + FRAME, :] = jnp.zeros((FRAME, CHAN), BF16)
        gp[3, WID : WID + FRAME, :] = jnp.zeros((FRAME, CHAN), BF16)

    SPAN = 64
    cell = lax.broadcasted_iota(jnp.int32, (SPAN, HD), 0) % WID

    def tap_sum(buf, lanes, frame, row, mirror):
        sums = [None, None, None]
        for a in range(3):
            for b in range(3):
                block = buf[frame + a, pl.ds(row + b * WID, SPAN), lanes].astype(F32)
                for c in range(3):
                    tap = 9 * a + 3 * b + c
                    tap = 26 - tap if mirror else tap
                    term = w[pl.ds(tap, 1), lanes] * block
                    sums[c] = term if sums[c] is None else sums[c] + term
        left = jnp.where(cell == 0, 0.0, pltpu.roll(sums[0], 1, 0))
        right = jnp.where(cell == WID - 1, 0.0, pltpu.roll(sums[2], SPAN - 1, 0))
        return sums[1] + left + right

    TILES = HALO_COLS // HD
    SPANS = FRAME // SPAN

    def conv_step(part, store):
        def step(i, carry):
            lanes = pl.ds(pl.multiple_of(part * HALO_COLS + (i // (2 * SPANS)) * HD, HD), HD)
            store(lanes, (i // SPANS) % 2, pl.multiple_of((i % SPANS) * SPAN, SPAN))
            return carry

        lax.fori_loop(0, TILES * 2 * SPANS, step, 0)

    def forward(part):
        def store(lanes, frame, row):
            pre = tap_sum(hp, lanes, frame, row, False)
            sig = 1.0 / (1.0 + jnp.exp(-pre))
            at = pl.ds(pl.multiple_of(frame * FRAME + row, SPAN), SPAN)
            ff_o[at, lanes] = (pre * sig).astype(BF16)
            grad = fg[at, lanes].astype(F32) * sig * (1.0 + pre * (1.0 - sig))
            gp[frame + 1, pl.ds(pl.multiple_of(row + WID, WID), SPAN), lanes] = grad.astype(BF16)

        halo_arrived(hidden[part])
        conv_step(part, store)

    def backward(part):
        def store(lanes, frame, row):
            at = pl.ds(pl.multiple_of(frame * FRAME + row, SPAN), SPAN)
            gh_o[at, lanes] = tap_sum(gp, lanes, frame, row, True).astype(BF16)

        halo_arrived(grads[part])
        conv_step(part, store)

    for i in range(HEADS_DEV):
        kt[head(i), :] = jnp.maximum(k[:, head(i)], 0).T
        qt[head(i), :] = jnp.maximum(q[:, head(i)], 0).T
    z1[0] = jnp.zeros((8, HD), F32)
    gz1[0] = jnp.zeros((8, HD), F32)
    srow[...] = jnp.zeros((8, TOK), F32)
    for copy in loads[2:]:
        copy.wait()
    ones = jnp.ones((8, TOK), BF16)
    arrived(round_sq)
    rrow[...] = lax.rsqrt(total(tp1[0], tp1, 8) * (1.0 / FEATURES) + EPS)
    scale_k = rrow[1:2, :]
    for i in range(HEADS_DEV):
        feat = (kt[head(i), :].astype(F32) * scale_k).astype(BF16)
        z1[0, pl.ds(i, 1), :] = nt(ones, feat)[0:1] * (1.0 / TOKENS)
        part = nn(feat, v[:, head(i)]) * (1.0 / TOKENS)
        kvp[head(i), :] = part
        kvs[head(i), :] = part.astype(BF16)
    round_z1 = plane_round(1, z1.at[0], z1)
    start(round_z1)
    round_kv1 = plane_scatter(0, kvs, kv1)
    start(round_kv1)

    rinv[...] = as_columns(rrow[...], 0, 2)
    scale_q = rinv[:, 0:HD]
    scale_k = rinv[:, HD : 2 * HD]
    for i in range(HEADS_DEV):
        fq[:, head(i)], fql[:, head(i)] = split(jnp.maximum(q[:, head(i)].astype(F32), 0.0) * scale_q)
        fk[:, head(i)] = (jnp.maximum(k[:, head(i)].astype(F32), 0.0) * scale_k).astype(BF16)
        qt[head(i), :] = (qt[head(i), :].astype(F32) * rrow[0:1, :]).astype(BF16)

    halo_start(hidden[4])
    forward(0)
    forward(1)
    forward(2)
    halo_start(hidden[5])
    arrived(round_z1)
    z2[0] = total(z1[0], z1, PLANE)
    round_z2 = ring_round(0, z2.at[0], z2)
    start(round_z2)
    arrived(round_kv1)
    kvc[...] = total(kvp[mine, :], kv1, PLANE)
    kv2[0] = kvc[...].astype(BF16)
    round_kv2 = ring_round(1, kv2.at[0], kv2)
    start(round_kv2)
    halo_start(hidden[6])


    forward(3)
    forward(4)
    halo_start(hidden[7])
    arrived(round_z2)
    zt[...] = total(z2[0], z2, NZ)
    for i in range(HEADS_DEV):
        key_sum = jnp.broadcast_to(zt[pl.ds(i, 1), :], (HD, HD)).astype(BF16)
        inv = 1.0 / (1.0 + nt(fq[:, head(i)], key_sum) * (1.0 / HD))
        dinv[:, head(i)] = inv
        grad, low = split(g[:, head(i)].astype(F32) * inv)
        gn[:, head(i)] = grad
        gnl[:, head(i)] = low
        part = nn(qt[head(i), :], grad) * (1.0 / TOKENS)
        gkp[head(i), :] = part
        gks[head(i), :] = part.astype(BF16)
    round_gk1 = plane_scatter(3, gks, gk1)
    start(round_gk1)

    arrived(round_kv2)
    kvb[mine, :] = total(kvc[...], kv2, NZ).astype(BF16)
    round_kv3 = plane_gather(2, kvb)
    start(round_kv3)
    halo_start(hidden[8])
    forward(5)
    halo_start(hidden[9])
    forward(6)

    arrived(round_gk1)
    gkc[...] = total(gkp[mine, :], gk1, PLANE)
    gk2[0] = gkc[...].astype(BF16)
    round_gk2 = ring_round(2, gk2.at[0], gk2)
    start(round_gk2)

    arrived(round_kv3)
    for i in range(HEADS_DEV):
        mat = kvb[head(i), :]
        inv = dinv[:, head(i)]
        att = (nn(fq[:, head(i)], mat) + nn(fql[:, head(i)], mat)) * inv
        att_o[:, head(i)] = att.astype(BF16)
        inner = row_sums(g[:, head(i)].astype(F32) * inv * att)
        srow[pl.ds(i, 1), :] = inner[0:1]
        gz1[0, pl.ds(i, 1), :] = nn(inner.astype(BF16), fq[:, head(i)])[0:1] * (-1.0 / HD / TOKENS)
    round_gz1 = plane_round(4, gz1.at[0], gz1)
    start(round_gz1)
    tp2[0] = jnp.broadcast_to(srow[0:1, :] + srow[1:2, :] + srow[2:3, :], (8, TOK))
    round_qi = tp_round(1, tp2)
    start(round_qi)
    stores[0].start()
    halo_start(grads[0])
    halo_start(grads[1])
    forward(7)
    forward(8)
    halo_start(grads[2])


    arrived(round_gk2)
    gkb[mine, :] = total(gkc[...], gk2, NZ).astype(BF16)
    round_gk3 = plane_gather(5, gkb)
    start(round_gk3)
    arrived(round_gz1)
    gz2[0] = total(gz1[0], gz1, PLANE)
    round_gz2 = ring_round(3, gz2.at[0], gz2)
    start(round_gz2)
    halo_start(grads[3])
    halo_start(grads[4])
    forward(9)
    stores[1].start()

    arrived(round_qi)
    scale_q = rinv[:, 0:HD]
    rowq = rrow[0:1, :]
    coef = as_columns(total(tp2[0], tp2, 8) * (rowq * rowq * (1.0 / FEATURES)), 0, 1)
    gden = as_columns(srow[...], 0, HEADS_DEV) * (-1.0 / HD)
    for i in range(HEADS_DEV):
        raw = q[:, head(i)].astype(F32)
        mat = kvb[head(i), :]
        grad = nt(gn[:, head(i)], mat) + nt(gnl[:, head(i)], mat) + gden[:, i * HD : (i + 1) * HD] * zt[pl.ds(i, 1), :]
        gq_o[:, head(i)] = (jnp.where(raw > 0, grad, 0.0) * scale_q - coef * raw).astype(BF16)
    stores[2].start()
    backward(0)
    halo_start(grads[5])
    backward(1)
    halo_start(grads[6])
    backward(2)

    for copy in sent[:SENT_EARLY]:
        copy.wait()
    halo_sent(0, hp)

    arrived(round_gk3)
    inner = None
    for i in range(HEADS_DEV):
        grad = nt(v[:, head(i)], gkb[head(i), :])
        gfk[:, head(i)] = grad
        prod = fk[:, head(i)].astype(F32) * grad
        inner = prod if inner is None else inner + prod
    inner = row_sums(inner)
    arrived(round_gz2)
    gzt[...] = total(gz2[0], gz2, NZ)
    for i in range(HEADS_DEV):
        high, low = split(jnp.broadcast_to(gzt[pl.ds(i, 1), :], (8, HD)))
        feat = fk[:, head(i)]
        inner = inner + nt(high, feat) + nt(low, feat)
    tp3[0] = inner
    round_ki = tp_round(2, tp3)
    start(round_ki)
    halo_start(grads[7])
    halo_start(grads[8])
    halo_start(grads[9])
    scale_k = rinv[:, HD : 2 * HD]
    for i in range(HEADS_DEV):
        gv_o[:, head(i)] = nn(fk[:, head(i)], gkb[head(i), :]).astype(BF16)
        grad = gfk[:, head(i)] + gzt[pl.ds(i, 1), :]
        gfk[:, head(i)] = jnp.where(k[:, head(i)].astype(F32) > 0, grad, 0.0) * scale_k
    stores[4].start()
    backward(3)
    backward(4)
    backward(5)
    backward(6)
    backward(7)
    backward(8)
    backward(9)
    stores[5].start()


    arrived(round_ki)
    rowk = rrow[1:2, :]
    coef = as_columns(total(tp3[0], tp3, 8) * (rowk * rowk * (1.0 / FEATURES)), 0, 1)
    for i in range(HEADS_DEV):
        gk_o[:, head(i)] = (gfk[:, head(i)] - coef * k[:, head(i)].astype(F32)).astype(BF16)
    stores[3].start()

    for copy in sent[SENT_EARLY:]:
        copy.wait()
    halo_sent(1, gp)
    for copy in stores:
        copy.wait()


def store_all(*refs):
    sem = refs[18]
    loads = [pltpu.make_async_copy(refs[i], refs[12 + i], sem.at[0, i]) for i in range(6)]
    stores = [pltpu.make_async_copy(refs[12 + i], refs[6 + i], sem.at[1, i]) for i in range(6)]
    for copy in loads:
        copy.start()
    for load, store in zip(loads, stores):
        load.wait()
        store.start()
    for copy in stores:
        copy.wait()


def body(query_act, key_act, value_act, hidden_act, conv_weight, attention_grad, feedforward_grad):
    att = jax.ShapeDtypeStruct((TOK, COLS), BF16)
    conv = jax.ShapeDtypeStruct((TOK, CHAN), BF16)

    def vmem(shape, dtype):
        return pltpu.VMEM(shape, dtype)

    def state():
        return [
            vmem((COLS, HD), F32),
            vmem((COLS, HD), BF16),
            vmem((PLANE, CHUNK, HD), BF16),
            vmem((CHUNK, HD), F32),
            vmem((NZ, CHUNK, HD), BF16),
            vmem((COLS, HD), BF16),
        ]

    narrow = lambda dtype: vmem((TOK, COLS), dtype)
    wide = lambda: vmem((TOK, CHAN), BF16)
    padded = lambda: vmem((4, PAD_ROWS, CHAN), BF16)
    dma = pltpu.SemaphoreType.DMA
    outs = pl.pallas_call(
        kernel,
        out_shape=(att, conv, att, att, att, conv),
        in_specs=[pl.BlockSpec(memory_space=pl.ANY)] * 7,
        out_specs=(pl.BlockSpec(memory_space=pl.ANY),) * 6,
        scratch_shapes=[
            narrow(BF16), narrow(BF16), narrow(BF16), narrow(BF16), wide(), vmem((27, CHAN), F32), padded(), padded(),
            narrow(BF16), wide(), narrow(BF16), narrow(BF16), narrow(BF16), wide(),
            *[narrow(BF16)] * 5, vmem((COLS, TOK), BF16), vmem((COLS, TOK), BF16),
            vmem((TOK, 2 * HD), F32), vmem((8, TOK), F32), vmem((8, TOK), F32), narrow(F32), narrow(F32),
            vmem((8, 8, TOK), F32), vmem((8, 8, TOK), F32), vmem((8, 8, TOK), F32),
            *state(), *state(),
            vmem((PLANE, 8, HD), F32), vmem((NZ, 8, HD), F32), vmem((8, HD), F32),
            vmem((PLANE, 8, HD), F32), vmem((NZ, 8, HD), F32), vmem((8, HD), F32),
            dma((8,)), dma((6,)),
            dma((3,)), dma((3,)), dma((6,)), dma((6,)), dma((4,)), dma((4,)),
            dma((2, 2)), dma((2, 2, HALO_PARTS)),
        ],
        compiler_params=pltpu.CompilerParams(
            collective_id=0, has_side_effects=True, vmem_limit_bytes=VMEM_LIMIT
        ),
        name="token_mixing",
    )(query_act, key_act, value_act, attention_grad, hidden_act, feedforward_grad, conv_weight)
    return pl.pallas_call(
        store_all,
        out_shape=(att, conv, att, att, att, conv),
        in_specs=[pl.BlockSpec(memory_space=pl.ANY)] * 6,
        out_specs=(pl.BlockSpec(memory_space=pl.ANY),) * 6,
        scratch_shapes=[narrow(BF16), wide(), narrow(BF16), narrow(BF16), narrow(BF16), wide(), dma((2, 6))],
        compiler_params=pltpu.CompilerParams(vmem_limit_bytes=VMEM_LIMIT),
        name="store_results",
    )(*outs)


def solution(mesh):
    in_specs = (
        P("seq", "tp"),
        P("seq", "tp"),
        P("seq", "tp"),
        P("seq", "tp"),
        P(None, "tp"),
        P("seq", "tp"),
        P("seq", "tp"),
    )
    out_specs = (P("seq", "tp"),) * 6
    return jax.shard_map(body, mesh=mesh, in_specs=in_specs, out_specs=out_specs, check_vma=False)
```
